128 devices in a mesh: section: 8 (over y, core), dp: 16 (over z, x).
Axes of the slice: x: 4, y: 4, z: 4, core: 2. Of those that a mesh axis runs over, the one named last changes fastest.
Arguments:
- section_inputs: bfloat16 [8, 8, 512, 16384], P('section', None, 'dp'), may hold values from -6 to 6
- top_grad: bfloat16 [8, 512, 16384], P(None, 'dp'), may hold values from -6 to 6
- weights: bfloat16 [8, 16384, 2, 128], P('section', 'dp'), may hold values from -6 to 6
- first_moment: float32 [8, 16384, 2, 128], P('section', 'dp'), may hold values from -12 to 12
- second_moment: float32 [8, 16384, 2, 128], P('section', 'dp'), may hold values from 1 to 20
- block_list: int32 [8, 16, 16], P('section', 'dp'), may hold values from 0 to 15
- block_owner: int32 [8, 16, 16, 1], P('section', 'dp'), may hold values from 0 to 15; in each aligned block of 16 rows (0 to 15, 16 to 31, ..., all dimensions but the last counted through in order) at most 2 rows name the same one
Outputs:
- new_weights: bfloat16 [8, 16384, 2, 128], P('section', 'dp')
- new_first: float32 [8, 16384, 2, 128], P('section', 'dp')
- new_second: float32 [8, 16384, 2, 128], P('section', 'dp')
- rollout_blocks: bfloat16 [8, 16, 16, 2, 128, 128], P('section', 'dp')
- rollout_ids: int32 [8, 16, 16, 2], P('section', 'dp')
The draws below stay inside these ranges and needn't reach their ends.
Inputs may be any that keep to these rules, and one draw needn't show every extreme that they name: `block_list`: a tile may be listed twice. `block_owner`: among the 16 entries of one device no owner is named more than 2 times, a bound that some block reaches.
All inputs are finite; a program needn't handle non-finite values.
Results may differ from the reference program's by a relative error of at most 0.035.
Values may be sent and summed in bfloat16 or wider, within the bound.
A program may use at most 192 MiB of HBM per device.

```python
import math
import jax
import jax.numpy as jnp
import numpy as np
from jax import lax

D = 16384
R = 128
BS = 128
MB = 8
TMB = 32
LIST = 16
CAP = 2
SECTIONS = 8
TOKENS = 512
BLK_DEV = 16
N_DP = 16


def plant(drawn, key, low, largest):
    longest = drawn.shape.index(max(drawn.shape))
    spots = []
    for shift in (0, 1):
        where = [jax.random.randint(jax.random.fold_in(key, axis), (), 0, length) for axis, length in enumerate(drawn.shape)]
        where[longest] = (where[longest] + shift) % drawn.shape[longest]
        spots.append(tuple(where))
    return drawn.at[spots[0]].set(low).at[spots[1]].set(largest)


def raised(drawn, own_key, source, target, blocks, factor):
    def block_of(position):
        return (jnp.arange(drawn.shape[position]) // (drawn.shape[position] // blocks)).reshape((-1,) + (1,) * (drawn.ndim - 1 - position))

    near = jax.random.permutation(own_key, blocks)[block_of(target)]
    second = (block_of(target) + blocks // 2) % blocks
    return jnp.where((block_of(source) == near) | (block_of(source) == second), factor * drawn, drawn)


def block_scale(stream_key, dims, cuts, least, top_value):
    loudness = 1.0
    for dim, shards_of in cuts:
        heights = jax.random.uniform(jax.random.fold_in(jax.random.fold_in(stream_key, 6), dim), (shards_of,), jnp.float32, least / len(cuts), top_value / len(cuts))
        loudness = loudness * jnp.repeat(jnp.exp(heights), dims[dim] // shards_of).reshape((-1,) + (1,) * (len(dims) - 1 - dim))
    return loudness


def shared_out(key, own, number, rows, number_of, top, reach, slope):
    ranking = jax.random.permutation(key, number_of)
    crowded, ordinary = load_shares(number_of, rows * top, reach, slope, True), load_shares(number_of, rows * top, reach, slope, False)
    places = jnp.arange(number_of)

    def named(sizes, offset_by):
        used = int((sizes > 0).sum())
        fixed = max(1, used // 4)
        shifted = fixed + (places - fixed + offset_by * (used - fixed)) % max(1, number_of - fixed)
        return jnp.zeros((number_of,), jnp.int32).at[ranking[jnp.where(places < fixed, places, shifted)]].set(jnp.asarray(sizes, jnp.int32))

    sizes = jnp.where(number % 4 == 0, named(crowded, number // 4), named(ordinary, number - number // 4 - 1))
    mixed = jax.random.permutation(jax.random.fold_in(own, 3), number_of)
    giver, sink = mixed[0:number_of // 2 * 2:2], mixed[1:number_of // 2 * 2:2]
    margin = jnp.minimum(sizes[giver] - 1, reach - sizes[sink]) // 2
    margin = jnp.where((giver == ranking[0]) | (sink == ranking[0]) | (sizes[sink] == 0), 0, jnp.maximum(margin, 0))
    shifted = jax.random.randint(jax.random.fold_in(own, 4), (number_of // 2,), 0, 1 << 20) % (margin + 1)
    sizes = sizes.at[giver].add(-shifted).at[sink].add(shifted)
    items = jnp.searchsorted(jnp.cumsum(sizes), jnp.arange(rows * top), side="right").astype(jnp.int32)
    listing = items.reshape(top, rows).T
    listing = listing[jax.random.permutation(jax.random.fold_in(own, 1), rows)]
    offset_by = jax.random.randint(jax.random.fold_in(own, 2), (rows, 1), 0, top)
    return jnp.take_along_axis(listing, (jnp.arange(top)[None, :] + offset_by) % top, axis=1)


def load_shares(count, total, limit, skew, full):
    loads = [(1 << 20) // math.isqrt(grade ** skew) + 1 for grade in range(1, count + 1)]
    largest = limit if full else min(limit, max(-(-total // count), total * loads[0] // sum(loads)))
    least = 1 if total - largest >= count - 1 else 0
    given, spare = [largest] + [least] * (count - 1), total - largest - least * (count - 1)
    while spare > 0:
        free = [i for i in range(1, count) if given[i] < largest] or [i for i in range(1, count) if given[i] < limit]
        mass, budget = sum([loads[i] for i in free]), spare
        for i in free:
            more = min(limit - given[i], max(1, budget * loads[i] // mass), spare)
            given[i] = given[i] + more
            spare = spare - more
    return np.array(given)


def gaussian(stream_key, dims, deviation, bound, split=(), kind=jnp.bfloat16):
    level = block_scale(stream_key, dims, split, -0.22, 0.18) if split else 1.0
    values = jax.random.normal(stream_key, dims, jnp.float32) * deviation * level
    return jnp.minimum(jnp.maximum(values, -bound), bound).astype(kind)


def bell_draw_with(own_key, shape, scale, reach, cuts, heavy, kind=jnp.bfloat16):
    result = scale * jax.random.normal(own_key, shape, jnp.float32)
    if cuts:
        result = result * block_scale(own_key, shape, cuts, -0.22, 0.18)
    return jnp.clip(raised(result, jax.random.fold_in(own_key, 3), *heavy), -reach, reach).astype(kind)


def setup_inputs(seed: int = 0) -> dict:
    key_list = jax.random.split(jax.random.key(seed), 8)
    section_inputs = bell_draw_with(key_list[0], (SECTIONS, MB, TOKENS, D), 1.0, 6.0, ((0, 8), (2, 16)), (2, 3, 16, 2.0))
    top_grad = bell_draw_with(key_list[1], (MB, TOKENS, D), 1.0, 6.0, ((1, 16),), (1, 2, 16, 2.0))
    weights = gaussian(key_list[2], (SECTIONS, D, 2, R), 1.0, 6.0, ((0, 8), (1, 16)))
    first_moment = gaussian(key_list[3], (SECTIONS, D, 2, R), 2.0, 12.0, ((0, 8), (1, 16)), jnp.float32)
    second_moment = jnp.clip(jnp.exp(math.log(20.0) - 2.9957323 * jax.random.uniform(key_list[4], (SECTIONS, D, 2, R), jnp.float32) ** block_scale(key_list[4], (SECTIONS, D, 2, R), ((0, 8), (1, 16)), -0.2, 0.2)), 1.0, 20.0)
    block_list = plant(jax.random.randint(key_list[5], (SECTIONS, N_DP, LIST), 0, BLK_DEV), jax.random.fold_in(key_list[5], 1), 0, BLK_DEV - 1).astype(jnp.int32)
    block_owner_keys = jax.random.split(jax.random.fold_in(key_list[6], 1), SECTIONS * N_DP * LIST // LIST)
    block_owner_turns = jax.random.permutation(jax.random.fold_in(key_list[6], 3), SECTIONS * N_DP * LIST // LIST)
    block_owner = jax.vmap(lambda own, number: shared_out(jax.random.fold_in(key_list[6], 2), own, number, LIST, N_DP, 1, CAP, 2))(block_owner_keys, block_owner_turns).reshape((SECTIONS, N_DP, LIST, 1))
    return {"section_inputs": section_inputs, "top_grad": top_grad, "weights": weights, "first_moment": first_moment, "second_moment": second_moment, "block_list": block_list, "block_owner": block_owner}


beta_one = 0.9
beta_two = 0.999
correct_one = 1.0 - 0.9 ** 10
correct_two = 1.0 - 0.999 ** 10
learn_rate = 0.01
decay_rate = 0.1
adam_eps = 1e-08

def group_rows(array):
    width_last = array.shape[-1]
    return array.reshape(MB, N_DP, TMB, width_last).transpose(1, 0, 2, 3).reshape(N_DP * 2, MB // 2 * TMB, width_last)

def partial_grad(pieces):
    h_part, g_part, out_part, mid_part = pieces
    grad_a = jnp.dot(h_part.T, mid_part, preferred_element_type=jnp.float32) * D ** (-0.5)
    grad_b = jnp.dot(g_part.T, out_part, preferred_element_type=jnp.float32) * R ** (-0.5)
    return jnp.stack([grad_a, grad_b], axis=1).astype(jnp.bfloat16)

def push_one(tiles, chosen, owners, sender):
    positions = jnp.arange(LIST, dtype=jnp.int32)
    same = (owners[None, :] == owners[:, None]) & (positions[None, :] < positions[:, None])
    place = lax.optimization_barrier(jnp.sum(same.astype(jnp.int32), axis=1))
    selector = (owners[None, None, :] == jnp.arange(N_DP, dtype=jnp.int32)[:, None, None]) & (place[None, None, :] == jnp.arange(CAP, dtype=jnp.int32)[None, :, None])
    picked = jnp.take(tiles, chosen, axis=0)
    sent = jnp.dot(selector.reshape(N_DP * CAP, LIST).astype(jnp.bfloat16), picked.reshape(LIST, BS * BS), preferred_element_type=jnp.float32)
    sent = sent.astype(jnp.bfloat16).reshape(N_DP, CAP, BS, BS)
    global_ids = sender * BLK_DEV + chosen + 1
    ids = lax.optimization_barrier(jnp.sum(selector.astype(jnp.int32) * global_ids[None, None, :], axis=2)) - 1
    return (sent, ids)

def reference(section_inputs, top_grad, weights, first_moment, second_moment, block_list, block_owner):
    grad = top_grad
    out_w, out_m, out_v, out_blocks, out_ids = ([], [], [], [], [])
    for section in range(SECTIONS - 1, -1, -1):
        h_flat = section_inputs[section].reshape(MB * TOKENS, D)
        g_flat = grad.reshape(MB * TOKENS, D)
        adapt_a = weights[section, :, 0, :]
        adapt_b = weights[section, :, 1, :]
        adapter_out = (jnp.dot(h_flat, adapt_a, preferred_element_type=jnp.float32) * D ** (-0.5)).astype(jnp.bfloat16)
        delta_mid = (jnp.dot(g_flat, adapt_b, preferred_element_type=jnp.float32) * R ** (-0.5)).astype(jnp.bfloat16)
        back = g_flat.astype(jnp.float32) + jnp.dot(delta_mid, adapt_a.T, preferred_element_type=jnp.float32) * D ** (-0.5)
        back = back.astype(jnp.bfloat16)

        def add_part(total, pieces):
            return (total + partial_grad(pieces).astype(jnp.float32), None)
        gradient, unused = lax.scan(add_part, jnp.zeros((D, 2, R), jnp.float32), (group_rows(h_flat), group_rows(g_flat), group_rows(adapter_out), group_rows(delta_mid)))
        new_first = beta_one * first_moment[section] + (1.0 - beta_one) * gradient
        new_second = beta_two * second_moment[section] + (1.0 - beta_two) * gradient * gradient
        master = weights[section].astype(jnp.float32)
        update = new_first / correct_one / (jnp.sqrt(new_second / correct_two) + adam_eps)
        new_w = (master - learn_rate * (update + decay_rate * master)).astype(jnp.bfloat16)
        tiles = new_w.reshape(N_DP, D // N_DP // BS, BS, 2, R // BS, BS).transpose(0, 1, 3, 4, 2, 5).reshape(N_DP, BLK_DEV, BS, BS)
        sent, ids = jax.vmap(push_one)(tiles, block_list[section], block_owner[section, :, :, 0], jnp.arange(N_DP, dtype=jnp.int32))
        out_w.append(new_w)
        out_m.append(new_first)
        out_v.append(new_second)
        out_blocks.append(sent.transpose(1, 0, 2, 3, 4))
        out_ids.append(ids.transpose(1, 0, 2))
        grad = back.reshape(MB, TOKENS, D)
    return (jnp.stack(out_w[::-1]), jnp.stack(out_m[::-1]), jnp.stack(out_v[::-1]), jnp.stack(out_blocks[::-1]), jnp.stack(out_ids[::-1]))
```

```python
import jax
import jax.numpy as jnp
from jax import lax
from jax.sharding import PartitionSpec as P

BS = 128
CAP = 2


beta_one = 0.9
beta_two = 0.999
correct_one = 1.0 - 0.9**10
correct_two = 1.0 - 0.999**10
learn_rate = 0.01
decay_rate = 0.1
adam_eps = 1e-08


def contract_rows(left, right):
    return lax.dot_general(
        left, right, (((0,), (0,)), ((), ())), preferred_element_type=jnp.float32
    )


def shards(section_inputs, top_grad, weights, first_moment, second_moment, block_list, block_owner):
    sections = lax.axis_size("section")
    section_pos = lax.axis_index("section")
    micro_count = section_inputs.shape[1]
    tok_rows = section_inputs.shape[2]
    model_width = section_inputs.shape[3]
    adapter_rank = weights.shape[3]
    scale_a = model_width ** (-0.5)
    scale_b = adapter_rank ** (-0.5)
    shard_rows = weights.shape[1]
    token_total = micro_count * tok_rows
    rows_a = weights[0, :, 0, :]
    rows_b = weights[0, :, 1, :]
    h_all = section_inputs[0].reshape(token_total, model_width)
    top_all = top_grad.reshape(token_total, model_width)
    every_a = lax.all_gather(rows_a, "section", axis=0)
    adapt_a = lax.all_gather(rows_a, "dp", axis=0, tiled=True)
    adapt_b = lax.all_gather(rows_b, "dp", axis=0, tiled=True)
    cross = lax.psum(
        lax.dot_general(every_a, rows_b, (((1,), (0,)), ((), ())), preferred_element_type=jnp.float32), "dp"
    )
    above = (jnp.arange(sections) > section_pos)[:, None, None]
    cross = jnp.where(above, cross * (scale_a * scale_b), 0.0).astype(jnp.bfloat16)
    adapter_out = (jnp.dot(h_all, adapt_a, preferred_element_type=jnp.float32) * scale_a).astype(jnp.bfloat16)
    direct = jnp.dot(top_all, adapt_b, preferred_element_type=jnp.float32) * scale_b
    every_direct = lax.all_gather(direct, "section", axis=0)
    every_cross = lax.all_gather(cross, "section", axis=0)
    deltas = [None] * sections
    for layer in range(sections - 1, -1, -1):
        total = every_direct[layer]
        for upper in range(layer + 1, sections):
            total = total + jnp.dot(deltas[upper], every_cross[layer, upper], preferred_element_type=jnp.float32)
        deltas[layer] = total.astype(jnp.bfloat16)
    deltas = jnp.stack(deltas)
    delta_mid = lax.dynamic_index_in_dim(deltas, section_pos, 0, keepdims=False)
    mixed = lax.psum(
        lax.dot_general(deltas, adapter_out, (((1,), (0,)), ((), ())), preferred_element_type=jnp.float32), "dp"
    )
    mixed = jnp.where(above, mixed, 0.0).astype(jnp.bfloat16)
    part_b = contract_rows(top_all, adapter_out).astype(jnp.bfloat16)
    part_a = contract_rows(h_all, delta_mid).astype(jnp.bfloat16)
    sum_b = lax.psum_scatter(part_b, "dp", scatter_dimension=0, tiled=True).astype(jnp.float32)
    sum_a = lax.psum_scatter(part_a, "dp", scatter_dimension=0, tiled=True).astype(jnp.float32)
    relayed = lax.dot_general(every_a, mixed, (((0, 2), (0, 1)), ((), ())), preferred_element_type=jnp.float32)
    gradient = jnp.stack([sum_a * scale_a, (sum_b + relayed * scale_a) * scale_b], axis=1)
    new_first = beta_one * first_moment[0] + (1.0 - beta_one) * gradient
    new_second = beta_two * second_moment[0] + (1.0 - beta_two) * gradient * gradient
    master = weights[0].astype(jnp.float32)
    update = new_first / correct_one / (jnp.sqrt(new_second / correct_two) + adam_eps)
    new_shard = (master - learn_rate * (update + decay_rate * master)).astype(jnp.bfloat16)
    row_blocks = shard_rows // BS
    col_blocks = adapter_rank // BS
    tiles = (
        new_shard.reshape(row_blocks, BS, 2, col_blocks, BS)
        .transpose(0, 2, 3, 1, 4)
        .reshape(-1, BS, BS)
    )
    tile_count = tiles.shape[0]
    chosen = block_list[0, 0]
    owners = block_owner[0, 0, :, 0]
    list_len = chosen.shape[0]
    dp_size = lax.axis_size("dp")
    positions = jnp.arange(list_len, dtype=jnp.int32)
    same_owner = (owners[None, :] == owners[:, None]) & (positions[None, :] < positions[:, None])
    place = jnp.sum(same_owner.astype(jnp.int32), axis=1)
    selector = (owners[None, None, :] == jnp.arange(dp_size, dtype=jnp.int32)[:, None, None]) & (
        place[None, None, :] == jnp.arange(CAP, dtype=jnp.int32)[None, :, None]
    )
    picked = jnp.take(tiles, chosen, axis=0)
    send_tiles = jnp.dot(
        selector.reshape(dp_size * CAP, list_len).astype(jnp.bfloat16),
        picked.reshape(list_len, BS * BS),
        preferred_element_type=jnp.float32,
    )
    send_tiles = send_tiles.astype(jnp.bfloat16).reshape(dp_size, CAP, BS, BS)
    global_ids = lax.axis_index("dp") * tile_count + chosen + 1
    send_ids = jnp.sum(selector.astype(jnp.int32) * global_ids[None, None, :], axis=2) - 1
    recv_tiles, recv_ids = (
        lax.all_to_all(send_tiles, "dp", split_axis=0, concat_axis=0, tiled=True),
        lax.all_to_all(send_ids, "dp", split_axis=0, concat_axis=0, tiled=True),
    )
    return (
        new_shard[None],
        new_first[None],
        new_second[None],
        recv_tiles[None, None],
        recv_ids[None, None],
    )


def solution(mesh):
    placed = (
        P("section", None, "dp", None),
        P(None, "dp", None),
        P("section", "dp", None, None),
        P("section", "dp", None, None),
        P("section", "dp", None, None),
        P("section", "dp", None),
        P("section", "dp", None, None),
    )
    return jax.shard_map(
        shards,
        mesh=mesh,
        in_specs=placed,
        out_specs=(
            P("section", "dp", None, None),
            P("section", "dp", None, None),
            P("section", "dp", None, None),
            P("section", "dp", None, None, None, None),
            P("section", "dp", None, None),
        ),
        check_vma=False,
    )
```

```python
import functools

import jax
import jax.numpy as jnp
from jax import lax
from jax.experimental import pallas as pl
from jax.experimental.pallas import tpu as pltpu
from jax.sharding import PartitionSpec as P

BS = 128
CAP = 2
RING = 4
GROUP = RING * RING

beta_one = 0.9
beta_two = 0.999
correct_one = 1.0 - 0.9**10
correct_two = 1.0 - 0.999**10
learn_rate = 0.01
decay_rate = 0.1
adam_eps = 1e-08

MESH = pl.DeviceIdType.MESH
F32 = jnp.float32
BF16 = jnp.bfloat16
DIRS = (1, -1)
SHIFTS = (0, 1, 3, 2)


def wrap(value):
    return lax.rem(value + 2 * RING, RING)


class Plane:
    def __init__(self):
        me = lax.axis_index("dp")
        self.me = me
        z, x = me // RING, lax.rem(me, RING)
        self.place = ((x, z), (z, x))

    def slot(self, half, first, second):
        i, j = self.place[half]
        i, j = wrap(i + first), wrap(j + second)
        return j * RING + i if half == 0 else i * RING + j

    def away(self, dz, dx):
        return self.slot(1, dz, dx)


class Gather:
    def __init__(self, plane, buf, send_sem, recv_sem):
        self.plane, self.buf, self.send_sem, self.recv_sem = plane, buf, send_sem, recv_sem
        self.rows = buf.shape[1]

    def part(self, half, piece):
        if piece is None:
            return pl.ds(half * (self.rows // 2), self.rows // 2)
        return pl.ds(half * (self.rows // 2) + piece * (self.rows // 4), self.rows // 4)

    def copy(self, half, kind, d, a, arriving):
        plane = self.plane
        dd = 0 if d == 1 else 1
        hop = -d if arriving else 0
        if kind == "F1":
            k, q, piece = dd, plane.slot(half, hop, 0), None
        elif kind == "F2":
            k, q, piece = 2 + dd, plane.slot(half, hop - d, 0), dd
        elif kind == "G1":
            k, q, piece = 4 + 2 * a + dd, plane.slot(half, a, hop), None
        else:
            k, q, piece = 12 + 2 * a + dd, plane.slot(half, a, hop - d), dd
        to = plane.slot(half, d, 0) if kind[0] == "F" else plane.slot(half, 0, d)
        where = self.buf.at[q, self.part(half, piece)]
        return pltpu.make_async_remote_copy(
            src_ref=where, dst_ref=where, send_sem=self.send_sem.at[0], recv_sem=self.recv_sem.at[half * 20 + k],
            device_id={"dp": to}, device_id_type=MESH,
        )

    def send(self, kind, a=0):
        for half in (0, 1):
            for d in DIRS:
                self.copy(half, kind, d, a, False).start()

    def wait(self, kind, a=0):
        for half in (0, 1):
            for d in DIRS:
                self.copy(half, kind, d, a, True).wait_recv()

    def round0(self):
        self.send("F1")
        self.send("G1", 0)

    def round1(self):
        self.wait("F1")
        self.send("F2")
        self.send("G1", 1)
        self.send("G1", 3)
        self.wait("G1", 0)
        self.send("G2", 0)
        return ((0, 0), (0, 1), (0, 3), (1, 0), (3, 0))

    def round2(self):
        self.wait("F2")
        self.send("G1", 2)
        self.wait("G1", 1)
        self.send("G2", 1)
        self.wait("G1", 3)
        self.send("G2", 3)
        self.wait("G2", 0)
        return ((1, 1), (1, 3), (3, 1), (3, 3), (2, 0), (0, 2))

    def round3(self):
        self.wait("G1", 2)
        self.send("G2", 2)
        self.wait("G2", 1)
        self.wait("G2", 3)
        return ((2, 1), (2, 3), (1, 2), (3, 2))

    def round4(self):
        self.wait("G2", 2)
        return ((2, 2),)

    def finish(self):
        whole = self.buf.at[pl.ds(0, GROUP - 1)]
        pltpu.make_async_remote_copy(
            src_ref=whole, dst_ref=whole, send_sem=self.send_sem.at[0], recv_sem=self.recv_sem.at[0],
            device_id={"dp": self.plane.slot(0, 1, 0)}, device_id_type=MESH,
        ).wait_send()


class Scatter:
    def __init__(self, plane, part, land, send_sem, recv_sem):
        self.plane, self.part, self.land = plane, part, land
        self.send_sem, self.recv_sem = send_sem, recv_sem
        self.quarter = part.shape[1] // 4

    def rows(self, half, piece):
        return pl.ds((2 * half + piece) * self.quarter, self.quarter)

    def index(self, half, kind, d, a):
        dd = 0 if d == 1 else 1
        base = {"S1": 0, "S2": 8, "S3": 16, "U1": 24, "U2": 26, "U3": 28}[kind]
        return half * 30 + base + (2 * a if kind[0] == "S" else 0) + dd

    def copy(self, half, kind, d, a):
        plane = self.plane
        dd = 0 if d == 1 else 1
        far = 2 if kind[1] == "1" else d
        piece = 1 - dd if kind[1] == "2" else dd
        if kind[0] == "S":
            q, to = plane.slot(half, a, far), plane.slot(half, 0, d)
        else:
            q, to = plane.slot(half, far, 0), plane.slot(half, d, 0)
        k = self.index(half, kind, d, a)
        return pltpu.make_async_remote_copy(
            src_ref=self.part.at[q, self.rows(half, piece)], dst_ref=self.land.at[k],
            send_sem=self.send_sem.at[0], recv_sem=self.recv_sem.at[k],
            device_id={"dp": to}, device_id_type=MESH,
        )

    def landed(self, half, kind, d, a=0):
        self.copy(half, kind, d, a).wait_recv()
        return self.land[self.index(half, kind, d, a)].astype(F32)

    def send_chunk(self, dz, dx):
        for half, a, far in ((0, dx, dz), (1, dz, dx)):
            if far == 2:
                for d in DIRS:
                    self.copy(half, "S1", d, a).start()
            elif far == 1:
                self.copy(half, "S2", 1, a).start()
            elif far == 3:
                self.copy(half, "S2", -1, a).start()

    def pass_on(self, a):
        for half in (0, 1):
            for d in DIRS:
                q, rows = self.plane.slot(half, a, d), self.rows(half, 0 if d == 1 else 1)
                total = self.part[q, rows].astype(F32) + self.landed(half, "S1", d, a)
                self.part[q, rows] = total.astype(BF16)
                self.copy(half, "S3", d, a).start()

    def settle(self, a):
        for half in (0, 1):
            q = self.plane.slot(half, a, 0)
            for piece, d in ((0, 1), (1, -1)):
                rows = self.rows(half, piece)
                total = self.part[q, rows].astype(F32) + self.landed(half, "S3", d, a) + self.landed(half, "S2", -d, a)
                self.part[q, rows] = total.astype(BF16)
            if a == 2:
                for d in DIRS:
                    self.copy(half, "U1", d, 0).start()
            elif a == 1:
                self.copy(half, "U2", 1, 0).start()
            elif a == 3:
                self.copy(half, "U2", -1, 0).start()

    def pass_last(self):
        for half in (0, 1):
            for d in DIRS:
                q, rows = self.plane.slot(half, d, 0), self.rows(half, 0 if d == 1 else 1)
                total = self.part[q, rows].astype(F32) + self.landed(half, "U1", d)
                self.part[q, rows] = total.astype(BF16)
                self.copy(half, "U3", d, 0).start()

    def result(self, total):
        me = self.plane.me
        for half in (0, 1):
            for piece, d in ((0, 1), (1, -1)):
                rows = self.rows(half, piece)
                total[rows] = (
                    self.part[me, rows].astype(F32) + self.landed(half, "U3", d) + self.landed(half, "U2", -d)
                )

    def finish(self):
        whole = self.part.at[pl.ds(0, GROUP - 1)]
        pltpu.make_async_remote_copy(
            src_ref=whole, dst_ref=whole, send_sem=self.send_sem.at[0], recv_sem=self.recv_sem.at[0],
            device_id={"dp": self.plane.slot(0, 1, 0)}, device_id_type=MESH,
        ).wait_send()


class Exchange:
    def __init__(self, plane, sems):
        self.plane, self.sems = plane, sems

    def copy(self, src, dst, to):
        return pltpu.make_async_remote_copy(
            src_ref=src, dst_ref=dst, send_sem=self.sems.at[0], recv_sem=self.sems.at[1],
            device_id={"dp": to}, device_id_type=MESH,
        )

    def start(self, src, dst):
        for k in range(1, GROUP):
            to = lax.rem(self.plane.me + k, GROUP)
            self.copy(src(to), dst(k), to).start()

    def wait_recv(self, whole):
        self.copy(whole, whole, lax.rem(self.plane.me + 1, GROUP)).wait_recv()

    def wait_send(self, whole):
        self.copy(whole, whole, lax.rem(self.plane.me + 1, GROUP)).wait_send()


def whole_kernel(
    sections, scale_a, scale_b,
    h_hbm, top_hbm, w_hbm, m_hbm, v_hbm, slot_ref, ids_ref,
    w_out, m_out, v_out, blocks_out, ids_out,
    h_v, top_v, w_v, wide, m_v, v_v,
    all_a, all_b, part_a, part_b, land_a, land_b,
    rows_a, cross_all, cross_part, cross_land, mixed_part, mixed_land, mixed,
    acc, out_t, out_n, u_all, u_acc, deltas, total, relayed, tiles, outbox, w_new, ids_in,
    local_sem, ga_send, ga_recv, gb_send, gb_recv, sa_send, sa_recv, sb_send, sb_recv,
    row_send, row_recv, cross_send, cross_recv, u_send, u_recv, swap_sem,
):
    s = lax.axis_index("section")
    plane = Plane()
    me = plane.me
    width = w_v.shape[0] // 2
    chunk = cross_part.shape[0] // GROUP
    rank = rows_a.shape[2]

    loads = [
        pltpu.make_async_copy(src, dst, local_sem.at[k])
        for k, (src, dst) in enumerate(((w_hbm, w_v), (h_hbm, h_v), (top_hbm, top_v), (m_hbm, m_v), (v_hbm, v_v)))
    ]
    for load in loads:
        load.start()

    barrier = pltpu.get_barrier_semaphore()
    for k in range(1, GROUP):
        pl.semaphore_signal(barrier, inc=1, device_id={"dp": lax.rem(me + k, GROUP)}, device_id_type=MESH)
    for k in range(1, sections):
        pl.semaphore_signal(barrier, inc=1, device_id={"section": lax.rem(s + k, sections)}, device_id_type=MESH)

    loads[0].wait()
    wide[...] = w_v[...].astype(F32)
    all_a[me] = wide[pl.ds(0, width, stride=2), :].astype(BF16)
    own_b = wide[pl.ds(1, width, stride=2), :]
    all_b[me] = own_b.astype(BF16)
    pl.semaphore_wait(barrier, GROUP - 1 + sections - 1)

    gather_a = Gather(plane, all_a, ga_send, ga_recv)
    gather_b = Gather(plane, all_b, gb_send, gb_recv)
    scatter_a = Scatter(plane, part_a, land_a, sa_send, sa_recv)
    scatter_b = Scatter(plane, part_b, land_b, sb_send, sb_recv)
    swap_cross = Exchange(plane, swap_sem.at[0])
    spread_cross = Exchange(plane, swap_sem.at[1])
    swap_mixed = Exchange(plane, swap_sem.at[2])
    spread_mixed = Exchange(plane, swap_sem.at[3])
    swap_ids = Exchange(plane, swap_sem.at[4])
    swap_tiles = Exchange(plane, swap_sem.at[5])

    def down(src, dst, send_sem, recv_sem, to):
        return pltpu.make_async_remote_copy(
            src_ref=src, dst_ref=dst, send_sem=send_sem, recv_sem=recv_sem,
            device_id={"section": to}, device_id_type=MESH,
        )

    def send_down(src, dst, send_sems, recv_sems):
        for to in range(sections - 2, -1, -1):
            @pl.when(to < s)
            def _():
                down(src, dst, send_sems.at[to], recv_sems.at[s], to).start()

    def sent_down(src, dst, send_sems, recv_sems):
        for to in range(sections - 2, -1, -1):
            @pl.when(to < s)
            def _():
                down(src, dst, send_sems.at[to], recv_sems.at[s], to).wait_send()

    def wait_above(block, send_sems, recv_sems):
        for layer in range(sections - 1, 0, -1):
            @pl.when(layer > s)
            def _():
                down(block(layer), block(layer), send_sems.at[layer], recv_sems.at[layer], layer).wait_recv()

    gather_a.round0()
    row_args = (all_a.at[me], rows_a.at[s], row_send, row_recv)
    send_down(*row_args)
    swap_ids.start(lambda q: ids_ref.at[q], lambda k: ids_in.at[me])
    ids_in[me] = ids_ref[me]
    for layer in range(sections):
        @pl.when(layer <= s)
        def _():
            rows_a[layer] = jnp.zeros(rows_a.shape[1:], BF16)
    own_bt = own_b.T.astype(BF16)

    gather_a.round1()

    wait_above(lambda layer: rows_a.at[layer], row_send, row_recv)
    for layer in range(sections):
        cross_part[layer * rank:(layer + 1) * rank] = jnp.dot(
            own_bt, rows_a[layer], preferred_element_type=F32
        ).astype(BF16)

    def piece(ref, q):
        return ref.at[pl.ds(pl.multiple_of(q * chunk, chunk), chunk)]

    swap_cross.start(lambda q: piece(cross_part, q), lambda k: cross_land.at[k - 1])
    gather_a.round2()
    gather_b.round0()
    gather_a.round3()

    swap_cross.wait_recv(cross_land)
    own_rows = pl.ds(pl.multiple_of(me * chunk, chunk), chunk)
    cross_sum = cross_part[own_rows].astype(F32)
    for k in range(GROUP - 1):
        cross_sum = cross_sum + cross_land[k].astype(F32)
    cross_all[s, own_rows] = (cross_sum * (scale_a * scale_b)).astype(BF16)
    spread_cross.start(lambda q: cross_all.at[s, own_rows], lambda k: cross_all.at[s, own_rows])

    gather_a.round4()
    loads[1].wait()

    def forward(left, blocks, q):
        cols = pl.ds(pl.multiple_of(q * width, width), width)
        return jnp.dot(left[:, cols], blocks[q], preferred_element_type=F32)

    acc[...] = jnp.zeros_like(acc)

    def forward_a(q, carry):
        acc[...] += forward(h_v, all_a, q)
        return carry

    lax.fori_loop(0, GROUP // 2, forward_a, 0)
    spots = gather_b.round1()
    lax.fori_loop(GROUP // 2, GROUP, forward_a, 0)
    adapter_out = acc[...] * scale_a
    out_n[...] = adapter_out.astype(BF16)
    out_t[...] = adapter_out.T.astype(BF16)
    loads[2].wait()

    spread_cross.wait_recv(cross_all.at[s, pl.ds(0, (GROUP - 1) * chunk)])
    cross_args = (cross_all.at[s], cross_all.at[s], cross_send, cross_recv)
    send_down(*cross_args)

    def backward(left, right, part, q):
        cols = pl.ds(pl.multiple_of(q * width, width), width)
        part[q] = jnp.dot(left, right[:, cols], preferred_element_type=F32).astype(BF16)

    def backward_b(q, carry):
        backward(out_t[...], top_v, part_b, q)
        return carry

    acc[...] = jnp.zeros_like(acc)

    def forward_b(spots):
        for dz, dx in spots:
            acc[...] += forward(top_v, all_b, plane.away(dz, dx))

    lax.fori_loop(0, GROUP // 2, backward_b, 0)
    forward_b(spots)
    spots = gather_b.round2()
    lax.fori_loop(GROUP // 2, GROUP, backward_b, 0)
    forward_b(spots)
    spots = gather_b.round3()
    order = [(2, 2)] + [(2, k) for k in (0, 1, 3)] + [(k, 2) for k in (0, 1, 3)]
    order += [(1, 1), (1, 3), (3, 1), (3, 3), (1, 0), (3, 0), (0, 1), (0, 3), (0, 0)]
    for dz, dx in order:
        scatter_b.send_chunk(dz, dx)
    forward_b(spots)
    forward_b(gather_b.round4())

    u_all[s] = (acc[...] * scale_b).T.astype(BF16)
    u_args = (u_all.at[s], u_all.at[s], u_send, u_recv)
    send_down(*u_args)
    wait_above(lambda layer: cross_all.at[layer], cross_send, cross_recv)
    wait_above(lambda layer: u_all.at[layer], u_send, u_recv)
    for layer in range(sections):
        @pl.when(layer >= s)
        def _():
            u_acc[layer] = u_all[layer].astype(F32)
    for layer in range(sections - 1, -1, -1):
        @pl.when(layer >= s)
        def _():
            delta = u_acc[layer].astype(BF16)
            deltas[layer] = delta
            for lower in range(layer):
                @pl.when(lower >= s)
                def _():
                    u_acc[lower] += jnp.dot(
                        cross_all[lower, layer * rank:(layer + 1) * rank], delta, preferred_element_type=F32
                    )

    for a in (2, 1, 3, 0):
        scatter_b.pass_on(a)

    for dz, dx in order:
        backward(deltas[s], h_v, part_a, plane.away(dz, dx))
        scatter_a.send_chunk(dz, dx)

    for layer in range(sections):
        @pl.when(layer > s)
        def _():
            mixed_part[layer * rank:(layer + 1) * rank] = jnp.dot(
                deltas[layer], out_n[...], preferred_element_type=F32
            ).astype(BF16)

        @pl.when(layer <= s)
        def _():
            mixed_part[layer * rank:(layer + 1) * rank] = jnp.zeros((rank, rank), BF16)
    swap_mixed.start(lambda q: piece(mixed_part, q), lambda k: mixed_land.at[k - 1])

    for a in (2, 1, 3, 0):
        scatter_b.settle(a)
    swap_mixed.wait_recv(mixed_land)
    mixed_sum = mixed_part[own_rows].astype(F32)
    for k in range(GROUP - 1):
        mixed_sum = mixed_sum + mixed_land[k].astype(F32)
    mixed[own_rows] = mixed_sum.astype(BF16)
    spread_mixed.start(lambda q: mixed.at[own_rows], lambda k: mixed.at[own_rows])
    scatter_b.pass_last()
    for a in (2, 1, 3, 0):
        scatter_a.pass_on(a)
    spread_mixed.wait_recv(mixed.at[pl.ds(0, (GROUP - 1) * chunk)])
    loads[3].wait()
    loads[4].wait()

    def adam(which, gradient_of):
        for block in range(width // BS):
            rows = pl.ds(2 * BS * block + which, BS, stride=2)
            gradient = gradient_of(pl.ds(block * BS, BS))
            new_first = beta_one * m_v[rows, :] + (1.0 - beta_one) * gradient
            new_second = beta_two * v_v[rows, :] + (1.0 - beta_two) * gradient * gradient
            master = wide[rows, :]
            update = new_first / correct_one / (jnp.sqrt(new_second / correct_two) + adam_eps)
            fresh = master - learn_rate * (update + decay_rate * master)
            m_v[rows, :] = new_first
            v_v[rows, :] = new_second
            wide[rows, :] = fresh
            tiles[2 * block + which] = fresh.astype(BF16)

    relayed[...] = jnp.dot(rows_a[0], mixed[0:rank], preferred_element_type=F32)
    for layer in range(1, sections):
        relayed[...] += jnp.dot(
            rows_a[layer], mixed[layer * rank:(layer + 1) * rank], preferred_element_type=F32
        )
    scatter_b.result(total)
    adam(1, lambda rows: (total[:, rows].T + relayed[rows] * scale_a) * scale_b)

    for a in (2, 1, 3, 0):
        scatter_a.settle(a)
    scatter_a.pass_last()
    scatter_a.result(total)
    adam(0, lambda rows: total[:, rows].T * scale_a)

    for k in range(GROUP * CAP):
        index = slot_ref[k // 128, k % 128]
        tile = tiles[jnp.maximum(index, 0)]
        outbox[k // CAP, k % CAP] = jnp.where(index >= 0, tile, jnp.zeros_like(tile))
    swap_tiles.start(lambda q: outbox.at[q], lambda k: blocks_out.at[me])
    kept = pltpu.make_async_copy(outbox.at[me], blocks_out.at[me], local_sem.at[5])
    kept.start()
    w_new[...] = wide[...].astype(BF16)
    stores = [
        pltpu.make_async_copy(src, dst, local_sem.at[k])
        for k, (src, dst) in enumerate(((w_new, w_out), (m_v, m_out), (v_v, v_out)))
    ]
    for store in stores:
        store.start()
    swap_ids.wait_recv(ids_in.at[pl.ds(0, GROUP - 1)])
    stores.append(pltpu.make_async_copy(ids_in, ids_out, local_sem.at[3]))
    stores[-1].start()

    gather_a.finish()
    gather_b.finish()
    scatter_a.finish()
    scatter_b.finish()
    sent_down(*row_args)
    sent_down(*cross_args)
    sent_down(*u_args)
    swap_ids.wait_send(ids_ref.at[pl.ds(0, GROUP - 1)])
    swap_cross.wait_send(cross_land)
    swap_mixed.wait_send(mixed_land)
    spread_cross.wait_send(mixed.at[pl.ds(0, (GROUP - 1) * chunk)])
    spread_mixed.wait_send(mixed.at[pl.ds(0, (GROUP - 1) * chunk)])
    swap_tiles.wait_send(outbox.at[pl.ds(0, GROUP - 1)])
    swap_tiles.wait_recv(blocks_out.at[pl.ds(0, GROUP - 1)])
    kept.wait()
    for store in stores:
        store.wait()


def shards(section_inputs, top_grad, weights, first_moment, second_moment, block_list, block_owner):
    sections = lax.axis_size("section")
    model_width = section_inputs.shape[3]
    rank = weights.shape[3]
    width = weights.shape[1]
    tokens = section_inputs.shape[1] * section_inputs.shape[2]
    chunk = sections * rank // GROUP
    scale_a = model_width ** (-0.5)
    scale_b = rank ** (-0.5)

    chosen = block_list[0, 0]
    owners = block_owner[0, 0, :, 0]
    positions = jnp.arange(chosen.shape[0], dtype=jnp.int32)
    same_owner = (owners[None, :] == owners[:, None]) & (positions[None, :] < positions[:, None])
    place = jnp.sum(same_owner.astype(jnp.int32), axis=1)
    selector = (owners[None, :] * CAP + place[None, :]) == jnp.arange(GROUP * CAP, dtype=jnp.int32)[:, None]
    slots = jnp.sum(jnp.where(selector, chosen[None, :] + 1, 0), axis=1) - 1
    tile_count = width * 2 // BS
    ids = jnp.where(slots >= 0, lax.axis_index("dp") * tile_count + slots, -1)
    ids = jnp.broadcast_to(ids.reshape(GROUP, 1, CAP), (GROUP, 8, CAP))
    ids = jnp.pad(ids, ((0, 0), (0, 0), (0, 128 - CAP)))
    slots = jnp.pad(slots[None], ((0, 0), (0, 128 - GROUP * CAP)))

    any_spec = pl.BlockSpec(memory_space=pl.ANY)
    vmem = pl.BlockSpec(memory_space=pltpu.VMEM)
    dma = pltpu.SemaphoreType.DMA
    new_weights, new_first, new_second, blocks, got_ids = pl.pallas_call(
        functools.partial(whole_kernel, sections, scale_a, scale_b),
        out_shape=(
            jax.ShapeDtypeStruct((2 * width, rank), BF16),
            jax.ShapeDtypeStruct((2 * width, rank), F32),
            jax.ShapeDtypeStruct((2 * width, rank), F32),
            jax.ShapeDtypeStruct((GROUP, CAP, BS, BS), BF16),
            jax.ShapeDtypeStruct((GROUP, 8, 128), jnp.int32),
        ),
        in_specs=[any_spec] * 5 + [pl.BlockSpec(memory_space=pltpu.SMEM), vmem],
        out_specs=(any_spec,) * 5,
        scratch_shapes=[
            pltpu.VMEM((tokens, model_width), BF16),
            pltpu.VMEM((tokens, model_width), BF16),
            pltpu.VMEM((2 * width, rank), BF16),
            pltpu.VMEM((2 * width, rank), F32),
            pltpu.VMEM((2 * width, rank), F32),
            pltpu.VMEM((2 * width, rank), F32),
            pltpu.VMEM((GROUP, width, rank), BF16),
            pltpu.VMEM((GROUP, width, rank), BF16),
            pltpu.VMEM((GROUP, rank, width), BF16),
            pltpu.VMEM((GROUP, rank, width), BF16),
            pltpu.VMEM((60, rank // 4, width), BF16),
            pltpu.VMEM((60, rank // 4, width), BF16),
            pltpu.VMEM((sections, width, rank), BF16),
            pltpu.VMEM((sections, sections * rank, rank), BF16),
            pltpu.VMEM((sections * rank, rank), BF16),
            pltpu.VMEM((GROUP - 1, chunk, rank), BF16),
            pltpu.VMEM((sections * rank, rank), BF16),
            pltpu.VMEM((GROUP - 1, chunk, rank), BF16),
            pltpu.VMEM((sections * rank, rank), BF16),
            pltpu.VMEM((tokens, rank), F32),
            pltpu.VMEM((rank, tokens), BF16),
            pltpu.VMEM((tokens, rank), BF16),
            pltpu.VMEM((sections, rank, tokens), BF16),
            pltpu.VMEM((sections, rank, tokens), F32),
            pltpu.VMEM((sections, rank, tokens), BF16),
            pltpu.VMEM((rank, width), F32),
            pltpu.VMEM((width, rank), F32),
            pltpu.VMEM((2 * width // BS, BS, BS), BF16),
            pltpu.VMEM((GROUP, CAP, BS, BS), BF16),
            pltpu.VMEM((2 * width, rank), BF16),
            pltpu.VMEM((GROUP, 8, 128), jnp.int32),
            dma((6,)),
            dma((1,)), dma((40,)), dma((1,)), dma((40,)),
            dma((1,)), dma((60,)), dma((1,)), dma((60,)),
            dma((sections,)), dma((sections,)),
            dma((sections,)), dma((sections,)),
            dma((sections,)), dma((sections,)),
            dma((6, 2)),
        ],
        compiler_params=pltpu.CompilerParams(
            collective_id=0, has_side_effects=True, vmem_limit_bytes=62 * 1024 * 1024
        ),
        cost_estimate=pl.CostEstimate(
            flops=8 * tokens * model_width * rank, bytes_accessed=4 * tokens * model_width, transcendentals=0
        ),
    )(
        section_inputs.reshape(tokens, model_width),
        top_grad.reshape(tokens, model_width),
        weights.reshape(2 * width, rank),
        first_moment.reshape(2 * width, rank),
        second_moment.reshape(2 * width, rank),
        slots,
        ids,
    )
    return (
        new_weights.reshape(weights.shape),
        new_first.reshape(weights.shape),
        new_second.reshape(weights.shape),
        blocks[None, None],
        got_ids[:, 0, :CAP][None, None],
    )


def solution(mesh):
    placed = (
        P("section", None, "dp", None),
        P(None, "dp", None),
        P("section", "dp", None, None),
        P("section", "dp", None, None),
        P("section", "dp", None, None),
        P("section", "dp", None),
        P("section", "dp", None, None),
    )
    return jax.shard_map(
        shards,
        mesh=mesh,
        in_specs=placed,
        out_specs=(
            P("section", "dp", None, None),
            P("section", "dp", None, None),
            P("section", "dp", None, None),
            P("section", "dp", None, None, None, None),
            P("section", "dp", None, None),
        ),
        check_vma=False,
    )
```

```python
import functools

import jax
import jax.numpy as jnp
from jax import lax
from jax.experimental import pallas as pl
from jax.experimental.pallas import tpu as pltpu
from jax.sharding import PartitionSpec as P

BS = 128
CAP = 2
RING = 4
GROUP = RING * RING

beta_one = 0.9
beta_two = 0.999
correct_one = 1.0 - 0.9**10
correct_two = 1.0 - 0.999**10
learn_rate = 0.01
decay_rate = 0.1
adam_eps = 1e-08

MESH = pl.DeviceIdType.MESH
F32 = jnp.float32
BF16 = jnp.bfloat16
DIRS = (1, -1)
SHIFTS = (0, 1, 3, 2)


def wrap(value):
    return lax.rem(value + 2 * RING, RING)


class Plane:
    def __init__(self):
        me = lax.axis_index("dp")
        self.me = me
        z, x = me // RING, lax.rem(me, RING)
        self.place = ((x, z), (z, x))

    def slot(self, half, first, second):
        i, j = self.place[half]
        i, j = wrap(i + first), wrap(j + second)
        return j * RING + i if half == 0 else i * RING + j

    def away(self, dz, dx):
        return self.slot(1, dz, dx)


class Gather:
    def __init__(self, plane, buf, send_sem, recv_sem):
        self.plane, self.buf, self.send_sem, self.recv_sem = plane, buf, send_sem, recv_sem
        self.rows = buf.shape[1]

    def part(self, half, piece):
        if piece is None:
            return pl.ds(half * (self.rows // 2), self.rows // 2)
        return pl.ds(half * (self.rows // 2) + piece * (self.rows // 4), self.rows // 4)

    def copy(self, half, kind, d, a, arriving):
        plane = self.plane
        dd = 0 if d == 1 else 1
        hop = -d if arriving else 0
        if kind == "F1":
            k, q, piece = dd, plane.slot(half, hop, 0), None
        elif kind == "F2":
            k, q, piece = 2 + dd, plane.slot(half, hop - d, 0), dd
        elif kind == "G1":
            k, q, piece = 4 + 2 * a + dd, plane.slot(half, a, hop), None
        else:
            k, q, piece = 12 + 2 * a + dd, plane.slot(half, a, hop - d), dd
        to = plane.slot(half, d, 0) if kind[0] == "F" else plane.slot(half, 0, d)
        where = self.buf.at[q, self.part(half, piece)]
        return pltpu.make_async_remote_copy(
            src_ref=where, dst_ref=where, send_sem=self.send_sem.at[0], recv_sem=self.recv_sem.at[half * 20 + k],
            device_id={"dp": to}, device_id_type=MESH,
        )

    def send(self, kind, a=0):
        for half in (0, 1):
            for d in DIRS:
                self.copy(half, kind, d, a, False).start()

    def wait(self, kind, a=0):
        for half in (0, 1):
            for d in DIRS:
                self.copy(half, kind, d, a, True).wait_recv()

    def round0(self):
        self.send("F1")
        self.send("G1", 0)

    def round1(self):
        self.wait("F1")
        self.send("F2")
        self.send("G1", 1)
        self.send("G1", 3)
        self.wait("G1", 0)
        self.send("G2", 0)
        return ((0, 0), (0, 1), (0, 3), (1, 0), (3, 0))

    def round2(self):
        self.wait("F2")
        self.send("G1", 2)
        self.wait("G1", 1)
        self.send("G2", 1)
        self.wait("G1", 3)
        self.send("G2", 3)
        self.wait("G2", 0)
        return ((1, 1), (1, 3), (3, 1), (3, 3), (2, 0), (0, 2))

    def round3(self):
        self.wait("G1", 2)
        self.send("G2", 2)
        self.wait("G2", 1)
        self.wait("G2", 3)
        return ((2, 1), (2, 3), (1, 2), (3, 2))

    def round4(self):
        self.wait("G2", 2)
        return ((2, 2),)

    def finish(self):
        whole = self.buf.at[pl.ds(0, GROUP - 1)]
        pltpu.make_async_remote_copy(
            src_ref=whole, dst_ref=whole, send_sem=self.send_sem.at[0], recv_sem=self.recv_sem.at[0],
            device_id={"dp": self.plane.slot(0, 1, 0)}, device_id_type=MESH,
        ).wait_send()


class Scatter:
    def __init__(self, plane, part, land, send_sem, recv_sem):
        self.plane, self.part, self.land = plane, part, land
        self.send_sem, self.recv_sem = send_sem, recv_sem
        self.quarter = part.shape[1] // 4

    def rows(self, half, piece):
        return pl.ds((2 * half + piece) * self.quarter, self.quarter)

    def index(self, half, kind, d, a):
        dd = 0 if d == 1 else 1
        base = {"S1": 0, "S2": 8, "S3": 16, "U1": 24, "U2": 26, "U3": 28}[kind]
        return half * 30 + base + (2 * a if kind[0] == "S" else 0) + dd

    def copy(self, half, kind, d, a):
        plane = self.plane
        dd = 0 if d == 1 else 1
        far = 2 if kind[1] == "1" else d
        piece = 1 - dd if kind[1] == "2" else dd
        if kind[0] == "S":
            q, to = plane.slot(half, a, far), plane.slot(half, 0, d)
        else:
            q, to = plane.slot(half, far, 0), plane.slot(half, d, 0)
        k = self.index(half, kind, d, a)
        return pltpu.make_async_remote_copy(
            src_ref=self.part.at[q, self.rows(half, piece)], dst_ref=self.land.at[k],
            send_sem=self.send_sem.at[0], recv_sem=self.recv_sem.at[k],
            device_id={"dp": to}, device_id_type=MESH,
        )

    def landed(self, half, kind, d, a=0):
        self.copy(half, kind, d, a).wait_recv()
        return self.land[self.index(half, kind, d, a)].astype(F32)

    def send_chunk(self, dz, dx):
        for half, a, far in ((0, dx, dz), (1, dz, dx)):
            if far == 2:
                for d in DIRS:
                    self.copy(half, "S1", d, a).start()
            elif far == 1:
                self.copy(half, "S2", 1, a).start()
            elif far == 3:
                self.copy(half, "S2", -1, a).start()

    def pass_on(self, a):
        for half in (0, 1):
            for d in DIRS:
                q, rows = self.plane.slot(half, a, d), self.rows(half, 0 if d == 1 else 1)
                total = self.part[q, rows].astype(F32) + self.landed(half, "S1", d, a)
                self.part[q, rows] = total.astype(BF16)
                self.copy(half, "S3", d, a).start()

    def settle(self, a):
        for half in (0, 1):
            q = self.plane.slot(half, a, 0)
            for piece, d in ((0, 1), (1, -1)):
                rows = self.rows(half, piece)
                total = self.part[q, rows].astype(F32) + self.landed(half, "S3", d, a) + self.landed(half, "S2", -d, a)
                self.part[q, rows] = total.astype(BF16)
            if a == 2:
                for d in DIRS:
                    self.copy(half, "U1", d, 0).start()
            elif a == 1:
                self.copy(half, "U2", 1, 0).start()
            elif a == 3:
                self.copy(half, "U2", -1, 0).start()

    def pass_last(self):
        for half in (0, 1):
            for d in DIRS:
                q, rows = self.plane.slot(half, d, 0), self.rows(half, 0 if d == 1 else 1)
                total = self.part[q, rows].astype(F32) + self.landed(half, "U1", d)
                self.part[q, rows] = total.astype(BF16)
                self.copy(half, "U3", d, 0).start()

    def result(self, total):
        me = self.plane.me
        for half in (0, 1):
            for piece, d in ((0, 1), (1, -1)):
                rows = self.rows(half, piece)
                total[rows] = (
                    self.part[me, rows].astype(F32) + self.landed(half, "U3", d) + self.landed(half, "U2", -d)
                )

    def finish(self):
        whole = self.part.at[pl.ds(0, GROUP - 1)]
        pltpu.make_async_remote_copy(
            src_ref=whole, dst_ref=whole, send_sem=self.send_sem.at[0], recv_sem=self.recv_sem.at[0],
            device_id={"dp": self.plane.slot(0, 1, 0)}, device_id_type=MESH,
        ).wait_send()


class Ring:
    def __init__(self, plane, buf, land, send_sem, recv_sem):
        self.plane, self.buf, self.land, self.send_sem, self.recv_sem = plane, buf, land, send_sem, recv_sem
        self.z = plane.place[1][0]
        self.half = buf.shape[1] // 2

    def piece(self, which):
        return pl.ds(which * self.half, self.half)

    def copy(self, src, dst, k, d):
        return pltpu.make_async_remote_copy(
            src_ref=src, dst_ref=dst, send_sem=self.send_sem.at[0], recv_sem=self.recv_sem.at[k],
            device_id={"dp": self.plane.slot(0, 0, d)}, device_id_type=MESH,
        )

    def gather_copy(self, kind, d, arriving):
        dd = 0 if d == 1 else 1
        hop = -d if arriving else 0
        if kind == 1:
            where = self.buf.at[wrap(self.z + hop)]
        else:
            where = self.buf.at[wrap(self.z + hop - d), self.piece(dd)]
        return self.copy(where, where, 2 * (kind - 1) + dd, d)

    def gather_send(self, kind):
        for d in DIRS:
            self.gather_copy(kind, d, False).start()

    def gather_wait(self, kind):
        for d in DIRS:
            self.gather_copy(kind, d, True).wait_recv()

    def sum_copy(self, kind, d):
        dd = 0 if d == 1 else 1
        far = 2 if kind == 1 else d
        k = 2 * (kind - 1) + dd
        src = self.buf.at[wrap(self.z + far), self.piece(1 - dd if kind == 2 else dd)]
        return self.copy(src, self.land.at[k], k, d)

    def landed(self, kind, d):
        self.sum_copy(kind, d).wait_recv()
        return self.land[2 * (kind - 1) + (0 if d == 1 else 1)].astype(F32)

    def sum_send(self):
        for kind in (1, 2):
            for d in DIRS:
                self.sum_copy(kind, d).start()

    def sum_pass(self):
        for d in DIRS:
            spot, rows = wrap(self.z + d), self.piece(0 if d == 1 else 1)
            self.buf[spot, rows] = (self.buf[spot, rows].astype(F32) + self.landed(1, d)).astype(BF16)
            self.sum_copy(3, d).start()

    def sum_result(self, total):
        for which, d in ((0, 1), (1, -1)):
            rows = self.piece(which)
            total[rows] = self.buf[self.z, rows].astype(F32) + self.landed(3, d) + self.landed(2, -d)

    def finish(self):
        whole = self.buf.at[pl.ds(0, RING - 1)]
        self.copy(whole, whole, 0, 1).wait_send()


class Exchange:
    def __init__(self, plane, sems):
        self.plane, self.sems = plane, sems

    def copy(self, src, dst, to):
        return pltpu.make_async_remote_copy(
            src_ref=src, dst_ref=dst, send_sem=self.sems.at[0], recv_sem=self.sems.at[1],
            device_id={"dp": to}, device_id_type=MESH,
        )

    def start(self, src, dst):
        for k in range(1, GROUP):
            to = lax.rem(self.plane.me + k, GROUP)
            self.copy(src(to), dst(k), to).start()

    def wait_recv(self, whole):
        self.copy(whole, whole, lax.rem(self.plane.me + 1, GROUP)).wait_recv()

    def wait_send(self, whole):
        self.copy(whole, whole, lax.rem(self.plane.me + 1, GROUP)).wait_send()


def whole_kernel(
    sections, scale_a, scale_b,
    h_hbm, top_hbm, w_hbm, m_hbm, v_hbm, list_ref, owner_ref,
    w_out, m_out, v_out, blocks_out, ids_out,
    h_v, w_v, wide, m_v, v_v,
    all_a, part_a, land_a, ring_b, slice_b, merged, u_part, u_land, u_turn, u_near, outs, grad_out, part_b, land_b,
    rows_a, cross_all, cross_part, cross_land, mixed_part, mixed_land, mixed,
    acc, out_n, u_all, u_acc, deltas, total, relayed, tiles, outbox, w_new, ids_in, ids_ref, slot_ref,
    local_sem, ga_send, ga_recv, gb_send, gb_recv, sa_send, sa_recv, sb_send, sb_recv,
    row_send, row_turn, row_recv, cross_send, cross_recv, u_send, u_turn_sem, u_recv, swap_sem, near_sem,
):
    s = lax.axis_index("section")
    plane = Plane()
    me = plane.me
    width = w_v.shape[0] // 2
    chunk = cross_part.shape[0] // GROUP
    rank = rows_a.shape[2]
    level, core = s // 2, lax.rem(s, 2)
    x = plane.place[0][0]
    tokens = h_v.shape[0]
    half_cols = pl.ds(pl.multiple_of(core * (width // 2), width // 2), width // 2)

    loads = [
        pltpu.make_async_copy(src, dst, local_sem.at[k])
        for k, (src, dst) in enumerate(((w_hbm, w_v), (h_hbm, h_v), (m_hbm, m_v), (v_hbm, v_v)))
    ]
    own_cols = pl.ds(pl.multiple_of((level * RING + x) * width, width), width)
    loads.append(pltpu.make_async_copy(top_hbm.at[:, own_cols], merged.at[x], local_sem.at[4]))
    for load in loads:
        load.start()

    barrier = pltpu.get_barrier_semaphore()
    for k in range(1, GROUP):
        pl.semaphore_signal(barrier, inc=1, device_id={"dp": lax.rem(me + k, GROUP)}, device_id_type=MESH)
    for k in range(1, sections):
        pl.semaphore_signal(barrier, inc=1, device_id={"section": lax.rem(s + k, sections)}, device_id_type=MESH)

    loads[0].wait()
    wide[...] = w_v[...].astype(F32)
    all_a[me] = wide[pl.ds(0, width, stride=2), :].astype(BF16)
    own_b = wide[pl.ds(1, width, stride=2), :]
    ring_b[plane.place[1][0]] = own_b.astype(BF16)
    pl.semaphore_wait(barrier, GROUP - 1 + sections - 1)

    gather_a = Gather(plane, all_a, ga_send, ga_recv)
    ring_gather = Ring(plane, ring_b, None, gb_send, gb_recv)
    scatter_a = Scatter(plane, part_a, land_a, sa_send, sa_recv)
    ring_sum = Ring(plane, part_b, land_b, sb_send, sb_recv)
    swap_cross = Exchange(plane, swap_sem.at[0])
    spread_cross = Exchange(plane, swap_sem.at[1])
    swap_mixed = Exchange(plane, swap_sem.at[2])
    spread_mixed = Exchange(plane, swap_sem.at[3])
    swap_ids = Exchange(plane, swap_sem.at[4])
    swap_tiles = Exchange(plane, swap_sem.at[5])

    def down(src, dst, send_sem, recv_sem, to):
        return pltpu.make_async_remote_copy(
            src_ref=src, dst_ref=dst, send_sem=send_sem, recv_sem=recv_sem,
            device_id={"section": to}, device_id_type=MESH,
        )

    def send_cross(waiting):
        for layer in range(1, sections - 1):
            @pl.when(s == layer)
            def _():
                block = cross_all.at[layer, pl.ds((layer + 1) * rank, (sections - 1 - layer) * rank)]
                for to in range(layer - 1, -1, -1):
                    copy = down(block, block, cross_send.at[to], cross_recv.at[layer], to)
                    if waiting:
                        copy.wait_send()
                    else:
                        copy.start()

    def wait_cross():
        for layer in range(1, sections - 1):
            @pl.when(layer > s)
            def _():
                block = cross_all.at[layer, pl.ds((layer + 1) * rank, (sections - 1 - layer) * rank)]
                down(block, block, cross_send.at[layer], cross_recv.at[layer], layer).wait_recv()

    class Cascade:
        def __init__(self, blocks, send_sem, turn_sem, recv_sem):
            self.blocks, self.send_sem, self.turn_sem, self.recv_sem = blocks, send_sem, turn_sem, recv_sem

        def copy(self, src, layer, sem, to):
            return down(src, self.blocks.at[layer], sem, self.recv_sem.at[layer], to)

        def outgoing(self, src, act):
            for to in range(sections // 2 - 2, -1, -1):
                @pl.when(to < level)
                def _():
                    act(self.copy(src, s, self.send_sem.at[to], 2 * to + core))

            @pl.when(core == 1)
            def _():
                act(self.copy(src, s, self.send_sem.at[RING - 1], s - 1))

        def send(self, src):
            self.outgoing(src, lambda copy: copy.start())

        def relay(self):
            for layer in range(sections - 1, 1, -1):
                @pl.when((layer // 2 > level) & (core == layer % 2))
                def _():
                    block = self.blocks.at[layer]
                    self.copy(block, layer, self.turn_sem.at[layer], s + 1 - 2 * core).wait_recv()
                    self.copy(block, layer, self.turn_sem.at[layer], s + 1 - 2 * core).start()

        def rest(self):
            for layer in range(sections - 1, 0, -1):
                @pl.when((layer > s) & ((layer // 2 == level) | (core != layer % 2)))
                def _():
                    block = self.blocks.at[layer]
                    self.copy(block, layer, self.turn_sem.at[layer], s + 1 - 2 * core).wait_recv()

        def finish(self, src):
            self.outgoing(src, lambda copy: copy.wait_send())
            for layer in range(sections - 1, 1, -1):
                @pl.when((layer // 2 > level) & (core == layer % 2))
                def _():
                    self.copy(self.blocks.at[layer], layer, self.turn_sem.at[layer], s + 1 - 2 * core).wait_send()

    row_cascade = Cascade(rows_a, row_send, row_turn, row_recv)
    u_cascade = Cascade(u_all, u_send, u_turn_sem, u_recv)

    def near(src, dst, group, k):
        to = plane.slot(0, k, 0)
        return pltpu.make_async_remote_copy(
            src_ref=src, dst_ref=dst, send_sem=near_sem.at[group, 0], recv_sem=near_sem.at[group, k],
            device_id={"dp": to}, device_id_type=MESH,
        )

    def across(src, dst, group, k):
        to = wrap(level + k) * 2 + core
        return pltpu.make_async_remote_copy(
            src_ref=src, dst_ref=dst, send_sem=near_sem.at[group, 0], recv_sem=near_sem.at[group, k],
            device_id={"section": to}, device_id_type=MESH,
        )

    def twin(src, dst, group, k):
        return pltpu.make_async_remote_copy(
            src_ref=src, dst_ref=dst, send_sem=near_sem.at[group, 0], recv_sem=near_sem.at[group, k],
            device_id={"section": s + 1 - 2 * core}, device_id_type=MESH,
        )

    HOPS = (1, 3, 2)

    def top_copy(k):
        cols = pl.ds(
            pl.multiple_of((level * RING + wrap(x + k)) * width + core * (width // 2), width // 2), width // 2
        )
        return near(top_hbm.at[:, cols], merged.at[x, :, half_cols], 0, k)

    ring_gather.gather_send(1)
    for k in HOPS:
        top_copy(k).start()
    gather_a.round0()
    row_cascade.send(all_a.at[me])

    entries = list_ref.shape[1]
    chosen = [list_ref[0, i] for i in range(entries)]
    owners = [owner_ref[0, i] for i in range(entries)]
    keys = []
    for i in range(entries):
        place = jnp.int32(0)
        for j in range(i):
            place += (owners[j] == owners[i]).astype(jnp.int32)
        keys.append(owners[i] * CAP + place)
    lane = lax.broadcasted_iota(jnp.int32, ids_ref.shape[1:], 1)

    def fill_slot(owner, carry):
        row = jnp.full(ids_ref.shape[1:], -1, jnp.int32)
        for place in range(CAP):
            index = jnp.int32(-1)
            for i in range(entries):
                index = jnp.where(keys[i] == owner * CAP + place, chosen[i], index)
            slot_ref[owner * CAP + place] = index
            row = jnp.where(lane == place, jnp.where(index >= 0, me * tiles.shape[0] + index, -1), row)
        ids_ref[owner] = row
        return carry

    lax.fori_loop(0, GROUP, fill_slot, 0)
    swap_ids.start(lambda q: ids_ref.at[q], lambda k: ids_in.at[me])
    ids_in[me] = ids_ref[me]
    for layer in range(sections):
        @pl.when(layer <= s)
        def _():
            rows_a[layer] = jnp.zeros(rows_a.shape[1:], BF16)
    own_bt = own_b.T.astype(BF16)

    ring_gather.gather_wait(1)
    ring_gather.gather_send(2)
    gather_a.round1()

    def passed_on(k):
        spot = merged.at[wrap(x - k), :, half_cols]
        return twin(spot, spot, 1, k)

    for k in HOPS:
        spot = merged.at[wrap(x - k), :, half_cols]
        near(spot, spot, 0, k).wait_recv()
        passed_on(k).start()
    ring_gather.gather_wait(2)
    for k in HOPS:
        across(ring_b.at[wrap(level + k)], slice_b.at[level], 2, k).start()
    slice_b[level] = ring_b[level]

    row_cascade.relay()
    row_cascade.rest()
    for layer in range(sections):
        cross_part[layer * rank:(layer + 1) * rank] = jnp.dot(
            own_bt, rows_a[layer], preferred_element_type=F32
        ).astype(BF16)

    def piece(ref, q):
        return ref.at[pl.ds(pl.multiple_of(q * chunk, chunk), chunk)]

    swap_cross.start(lambda q: piece(cross_part, q), lambda k: cross_land.at[k - 1])
    gather_a.round2()

    loads[4].wait()
    other_cols = pl.ds(pl.multiple_of((1 - core) * (width // 2), width // 2), width // 2)
    for k in HOPS:
        spot = merged.at[wrap(x - k), :, other_cols]
        twin(spot, spot, 1, k).wait_recv()

    def direct(layer_level, dst):
        for spot in range(RING):
            dst[spot] = jnp.dot(merged[spot], slice_b[layer_level], preferred_element_type=F32).astype(BF16)

    for n, k in enumerate(HOPS):
        across(slice_b.at[wrap(level - k)], slice_b.at[wrap(level - k)], 2, k).wait_recv()
        direct(wrap(level - k), u_part.at[n])
        across(u_part.at[n], u_land.at[n], 3, RING - k).start()
    direct(level, u_part.at[RING - 1])
    gather_a.round3()

    swap_cross.wait_recv(cross_land)
    own_rows = pl.ds(pl.multiple_of(me * chunk, chunk), chunk)
    cross_sum = cross_part[own_rows].astype(F32)
    for k in range(GROUP - 1):
        cross_sum = cross_sum + cross_land[k].astype(F32)
    cross_all[s, own_rows] = (cross_sum * (scale_a * scale_b)).astype(BF16)
    spread_cross.start(lambda q: cross_all.at[s, own_rows], lambda k: cross_all.at[s, own_rows])

    gather_a.round4()
    loads[1].wait()

    def forward(left, blocks, q):
        cols = pl.ds(pl.multiple_of(q * width, width), width)
        return jnp.dot(left[:, cols], blocks[q], preferred_element_type=F32)

    acc[...] = jnp.zeros_like(acc)

    def forward_a(q, carry):
        acc[...] += forward(h_v, all_a, q)
        return carry

    lax.fori_loop(0, GROUP // 2, forward_a, 0)

    for n, k in enumerate(HOPS):
        across(u_part.at[n], u_land.at[n], 3, RING - k).wait_recv()

    def turn(spot):
        summed = u_part[RING - 1, spot].astype(F32)
        for n in range(RING - 1):
            summed = summed + u_land[n, spot].astype(F32)
        return summed

    def u_copy(k):
        return near(u_turn.at[k - 1], u_near.at[k - 1], 4, k)

    for k in HOPS:
        u_turn[k - 1] = turn(wrap(x + k)).astype(BF16)
        u_copy(k).start()
    lax.fori_loop(GROUP // 2, GROUP, forward_a, 0)
    adapter_out = acc[...] * scale_a
    out_n[...] = adapter_out.astype(BF16)
    outs[level, x] = adapter_out.T.astype(BF16)
    for k in HOPS:
        near(outs.at[level, x], outs.at[level, x], 5, k).start()

    spread_cross.wait_recv(cross_all.at[s, pl.ds(0, (GROUP - 1) * chunk)])
    send_cross(False)

    def backward(left, right, part, q):
        cols = pl.ds(pl.multiple_of(q * width, width), width)
        part[q] = jnp.dot(left, right[:, cols], preferred_element_type=F32).astype(BF16)

    order = [(2, 2)] + [(2, k) for k in (0, 1, 3)] + [(k, 2) for k in (0, 1, 3)]
    order += [(1, 1), (1, 3), (3, 1), (3, 3), (1, 0), (3, 0), (0, 1), (0, 3), (0, 0)]
    own_direct = turn(x)
    for k in HOPS:
        u_copy(k).wait_recv()
        own_direct = own_direct + u_near[k - 1].astype(F32)

    u_all[s] = (own_direct * scale_b).T.astype(BF16)
    u_cascade.send(u_all.at[s])
    for k in HOPS:
        spot = outs.at[level, wrap(x - k)]
        near(spot, spot, 5, k).wait_recv()
    for k in HOPS:
        across(outs.at[level], outs.at[level], 6, k).start()
    wait_cross()
    u_cascade.relay()
    u_cascade.rest()
    for layer in range(sections):
        @pl.when(layer >= s)
        def _():
            u_acc[layer] = u_all[layer].astype(F32)
    for layer in range(sections - 1, -1, -1):
        @pl.when(layer >= s)
        def _():
            delta = u_acc[layer].astype(BF16)
            deltas[layer] = delta
            for lower in range(layer):
                @pl.when(lower >= s)
                def _():
                    u_acc[lower] += jnp.dot(
                        cross_all[lower, layer * rank:(layer + 1) * rank], delta, preferred_element_type=F32
                    )

    for dz, dx in order:
        backward(deltas[s], h_v, part_a, plane.away(dz, dx))
        scatter_a.send_chunk(dz, dx)

    for layer in range(sections):
        @pl.when(layer > s)
        def _():
            mixed_part[layer * rank:(layer + 1) * rank] = jnp.dot(
                deltas[layer], out_n[...], preferred_element_type=F32
            ).astype(BF16)

        @pl.when(layer <= s)
        def _():
            mixed_part[layer * rank:(layer + 1) * rank] = jnp.zeros((rank, rank), BF16)
    swap_mixed.start(lambda q: piece(mixed_part, q), lambda k: mixed_land.at[k - 1])

    def top_grad_of(layer_level):
        summed = jnp.dot(outs[layer_level, 0], merged[0], preferred_element_type=F32)
        for spot in range(1, RING):
            summed = summed + jnp.dot(outs[layer_level, spot], merged[spot], preferred_element_type=F32)
        return summed.astype(BF16)

    for n, k in enumerate(HOPS):
        spot = outs.at[wrap(level - k)]
        across(spot, spot, 6, k).wait_recv()
        grad_out[n] = top_grad_of(wrap(level - k))
        across(grad_out.at[n], part_b.at[level], 7, RING - k).start()
    part_b[level] = top_grad_of(level)
    swap_mixed.wait_recv(mixed_land)
    mixed_sum = mixed_part[own_rows].astype(F32)
    for k in range(GROUP - 1):
        mixed_sum = mixed_sum + mixed_land[k].astype(F32)
    mixed[own_rows] = mixed_sum.astype(BF16)
    spread_mixed.start(lambda q: mixed.at[own_rows], lambda k: mixed.at[own_rows])
    for a in (2, 1, 3, 0):
        scatter_a.pass_on(a)
    for k in HOPS:
        spot = part_b.at[wrap(level - k)]
        across(spot, spot, 7, k).wait_recv()
    ring_sum.sum_send()
    for a in (2, 1, 3, 0):
        scatter_a.settle(a)
    ring_sum.sum_pass()
    scatter_a.pass_last()
    spread_mixed.wait_recv(mixed.at[pl.ds(0, (GROUP - 1) * chunk)])
    loads[2].wait()
    loads[3].wait()

    def adam(which, gradient_of):
        for block in range(width // BS):
            rows = pl.ds(2 * BS * block + which, BS, stride=2)
            gradient = gradient_of(pl.ds(block * BS, BS))
            new_first = beta_one * m_v[rows, :] + (1.0 - beta_one) * gradient
            new_second = beta_two * v_v[rows, :] + (1.0 - beta_two) * gradient * gradient
            master = wide[rows, :]
            update = new_first / correct_one / (jnp.sqrt(new_second / correct_two) + adam_eps)
            fresh = master - learn_rate * (update + decay_rate * master)
            m_v[rows, :] = new_first
            v_v[rows, :] = new_second
            wide[rows, :] = fresh
            tiles[2 * block + which] = fresh.astype(BF16)

    relayed[...] = jnp.dot(rows_a[0], mixed[0:rank], preferred_element_type=F32)
    for layer in range(1, sections):
        relayed[...] += jnp.dot(
            rows_a[layer], mixed[layer * rank:(layer + 1) * rank], preferred_element_type=F32
        )
    ring_sum.sum_result(total)
    adam(1, lambda rows: (total[:, rows].T + relayed[rows] * scale_a) * scale_b)

    scatter_a.result(total)
    adam(0, lambda rows: total[:, rows].T * scale_a)

    for k in range(GROUP * CAP):
        index = slot_ref[k]
        tile = tiles[jnp.maximum(index, 0)]
        outbox[k // CAP, k % CAP] = jnp.where(index >= 0, tile, jnp.zeros_like(tile))
    swap_tiles.start(lambda q: outbox.at[q], lambda k: blocks_out.at[me])
    kept = pltpu.make_async_copy(outbox.at[me], blocks_out.at[me], local_sem.at[5])
    kept.start()
    w_new[...] = wide[...].astype(BF16)
    stores = [
        pltpu.make_async_copy(src, dst, local_sem.at[k])
        for k, (src, dst) in enumerate(((w_new, w_out), (m_v, m_out), (v_v, v_out)))
    ]
    for store in stores:
        store.start()
    swap_ids.wait_recv(ids_in.at[pl.ds(0, GROUP - 1)])
    stores.append(pltpu.make_async_copy(ids_in, ids_out, local_sem.at[3]))
    stores[-1].start()

    gather_a.finish()
    ring_gather.finish()
    scatter_a.finish()
    ring_sum.finish()
    for group, whole in (
        (0, merged.at[pl.ds(0, RING - 1), :, half_cols]), (1, merged.at[pl.ds(0, RING - 1), :, half_cols]),
        (2, slice_b.at[pl.ds(0, RING - 1)]), (3, u_land), (4, u_near),
        (5, outs.at[0, pl.ds(0, RING - 1)]), (6, outs.at[pl.ds(0, RING - 1)]), (7, grad_out),
    ):
        near(whole, whole, group, 1).wait_send()
    row_cascade.finish(all_a.at[me])
    send_cross(True)
    u_cascade.finish(u_all.at[s])
    swap_ids.wait_send(ids_ref.at[pl.ds(0, GROUP - 1)])
    swap_cross.wait_send(cross_land)
    swap_mixed.wait_send(mixed_land)
    spread_cross.wait_send(mixed.at[pl.ds(0, (GROUP - 1) * chunk)])
    spread_mixed.wait_send(mixed.at[pl.ds(0, (GROUP - 1) * chunk)])
    swap_tiles.wait_send(outbox.at[pl.ds(0, GROUP - 1)])
    swap_tiles.wait_recv(blocks_out.at[pl.ds(0, GROUP - 1)])
    kept.wait()
    for store in stores:
        store.wait()


def hand_over(
    w_in, m_in, v_in, blocks_in, ids_in, w_out, m_out, v_out, blocks_out, ids_out, w_v, m_v, v_v, blocks_v, in_sem, out_sem
):
    arrays = ((m_in, m_v, m_out), (v_in, v_v, v_out), (blocks_in, blocks_v, blocks_out), (w_in, w_v, w_out))
    fetches, stores = [], []
    for array, (src, stage, dst) in enumerate(arrays):
        half = src.shape[0] // 2
        for k in range(2):
            part = pl.ds(k * half, half)
            fetches.append(pltpu.make_async_copy(src.at[part], stage.at[part], in_sem.at[2 * array + k]))
            stores.append(pltpu.make_async_copy(stage.at[part], dst.at[part], out_sem.at[2 * array + k]))
    for fetch in fetches:
        fetch.start()
    ids_out[...] = ids_in[:, 0, :].T[:CAP, :]
    for fetch, store in zip(fetches, stores):
        fetch.wait()
        store.start()
    for store in stores:
        store.wait()


def shards(section_inputs, top_grad, weights, first_moment, second_moment, block_list, block_owner):
    sections = lax.axis_size("section")
    model_width = section_inputs.shape[3]
    rank = weights.shape[3]
    width = weights.shape[1]
    tokens = section_inputs.shape[1] * section_inputs.shape[2]
    chunk = sections * rank // GROUP
    entries = block_list.shape[2]
    scale_a = model_width ** (-0.5)
    scale_b = rank ** (-0.5)

    any_spec = pl.BlockSpec(memory_space=pl.ANY)
    vmem = pl.BlockSpec(memory_space=pltpu.VMEM)
    dma = pltpu.SemaphoreType.DMA
    new_weights, new_first, new_second, blocks, got_ids = pl.pallas_call(
        functools.partial(whole_kernel, sections, scale_a, scale_b),
        out_shape=(
            jax.ShapeDtypeStruct((2 * width, rank), BF16),
            jax.ShapeDtypeStruct((2 * width, rank), F32),
            jax.ShapeDtypeStruct((2 * width, rank), F32),
            jax.ShapeDtypeStruct((GROUP, CAP, BS, BS), BF16),
            jax.ShapeDtypeStruct((GROUP, 8, 128), jnp.int32),
        ),
        in_specs=[any_spec] * 5 + [pl.BlockSpec(memory_space=pltpu.SMEM)] * 2,
        out_specs=(any_spec,) * 5,
        scratch_shapes=[
            pltpu.VMEM((tokens, model_width), BF16),
            pltpu.VMEM((2 * width, rank), BF16),
            pltpu.VMEM((2 * width, rank), F32),
            pltpu.VMEM((2 * width, rank), F32),
            pltpu.VMEM((2 * width, rank), F32),
            pltpu.VMEM((GROUP, width, rank), BF16),
            pltpu.VMEM((GROUP, rank, width), BF16),
            pltpu.VMEM((60, rank // 4, width), BF16),
            pltpu.VMEM((RING, width, rank), BF16),
            pltpu.VMEM((RING, width, rank), BF16),
            pltpu.VMEM((RING, tokens, width), BF16),
            pltpu.VMEM((RING, RING, tokens, rank), BF16),
            pltpu.VMEM((RING - 1, RING, tokens, rank), BF16),
            pltpu.VMEM((RING - 1, tokens, rank), BF16),
            pltpu.VMEM((RING - 1, tokens, rank), BF16),
            pltpu.VMEM((RING, RING, rank, tokens), BF16),
            pltpu.VMEM((RING - 1, rank, width), BF16),
            pltpu.VMEM((RING, rank, width), BF16),
            pltpu.VMEM((6, rank // 2, width), BF16),
            pltpu.VMEM((sections, width, rank), BF16),
            pltpu.VMEM((sections, sections * rank, rank), BF16),
            pltpu.VMEM((sections * rank, rank), BF16),
            pltpu.VMEM((GROUP - 1, chunk, rank), BF16),
            pltpu.VMEM((sections * rank, rank), BF16),
            pltpu.VMEM((GROUP - 1, chunk, rank), BF16),
            pltpu.VMEM((sections * rank, rank), BF16),
            pltpu.VMEM((tokens, rank), F32),
            pltpu.VMEM((tokens, rank), BF16),
            pltpu.VMEM((sections, rank, tokens), BF16),
            pltpu.VMEM((sections, rank, tokens), F32),
            pltpu.VMEM((sections, rank, tokens), BF16),
            pltpu.VMEM((rank, width), F32),
            pltpu.VMEM((width, rank), F32),
            pltpu.VMEM((2 * width // BS, BS, BS), BF16),
            pltpu.VMEM((GROUP, CAP, BS, BS), BF16),
            pltpu.VMEM((2 * width, rank), BF16),
            pltpu.VMEM((GROUP, 8, 128), jnp.int32),
            pltpu.VMEM((GROUP, 8, 128), jnp.int32),
            pltpu.SMEM((GROUP * CAP,), jnp.int32),
            dma((6,)),
            dma((1,)), dma((40,)), dma((1,)), dma((4,)),
            dma((1,)), dma((60,)), dma((1,)), dma((6,)),
            dma((RING,)), dma((sections,)), dma((sections,)),
            dma((sections,)), dma((sections,)),
            dma((RING,)), dma((sections,)), dma((sections,)),
            dma((6, 2)), dma((8, RING)),
        ],
        compiler_params=pltpu.CompilerParams(
            collective_id=0, has_side_effects=True, vmem_limit_bytes=62 * 1024 * 1024
        ),
        cost_estimate=pl.CostEstimate(
            flops=8 * tokens * model_width * rank, bytes_accessed=4 * tokens * model_width, transcendentals=0
        ),
    )(
        section_inputs.reshape(tokens, model_width),
        top_grad.reshape(tokens, model_width),
        weights.reshape(2 * width, rank),
        first_moment.reshape(2 * width, rank),
        second_moment.reshape(2 * width, rank),
        block_list.reshape(1, entries),
        block_owner.reshape(1, entries),
    )
    results = (new_weights, new_first, new_second, blocks)
    *results, got_ids = pl.pallas_call(
        hand_over,
        out_shape=(
            *(jax.ShapeDtypeStruct(array.shape, array.dtype) for array in results),
            jax.ShapeDtypeStruct((CAP, GROUP), jnp.int32),
        ),
        in_specs=[any_spec] * 4 + [vmem],
        out_specs=(any_spec,) * 4 + (vmem,),
        scratch_shapes=[pltpu.VMEM(array.shape, array.dtype) for array in results] + [dma((8,)), dma((8,))],
    )(*results, got_ids)
    new_weights, new_first, new_second, blocks = results
    return (
        new_weights.reshape(weights.shape),
        new_first.reshape(weights.shape),
        new_second.reshape(weights.shape),
        blocks[None, None],
        got_ids.T[None, None],
    )


def solution(mesh):
    placed = (
        P("section", None, "dp", None),
        P(None, "dp", None),
        P("section", "dp", None, None),
        P("section", "dp", None, None),
        P("section", "dp", None, None),
        P("section", "dp", None),
        P("section", "dp", None, None),
    )
    return jax.shard_map(
        shards,
        mesh=mesh,
        in_specs=placed,
        out_specs=(
            P("section", "dp", None, None),
            P("section", "dp", None, None),
            P("section", "dp", None, None),
            P("section", "dp", None, None, None, None),
            P("section", "dp", None, None),
        ),
        check_vma=False,
    )
```

```python
import functools

import jax
import jax.numpy as jnp
from jax import lax
from jax.experimental import pallas as pl
from jax.experimental.pallas import tpu as pltpu
from jax.sharding import PartitionSpec as P

BS = 128
CAP = 2
RING = 4
GROUP = RING * RING

beta_one = 0.9
beta_two = 0.999
correct_one = 1.0 - 0.9**10
correct_two = 1.0 - 0.999**10
learn_rate = 0.01
decay_rate = 0.1
adam_eps = 1e-08

MESH = pl.DeviceIdType.MESH
F32 = jnp.float32
BF16 = jnp.bfloat16
DIRS = (1, -1)
SHIFTS = (0, 1, 3, 2)


def wrap(value):
    return lax.rem(value + 2 * RING, RING)


class Plane:
    def __init__(self):
        me = lax.axis_index("dp")
        self.me = me
        z, x = me // RING, lax.rem(me, RING)
        self.place = ((x, z), (z, x))

    def slot(self, half, first, second):
        i, j = self.place[half]
        i, j = wrap(i + first), wrap(j + second)
        return j * RING + i if half == 0 else i * RING + j

    def away(self, dz, dx):
        return self.slot(1, dz, dx)


class Gather:
    def __init__(self, plane, buf, send_sem, recv_sem):
        self.plane, self.buf, self.send_sem, self.recv_sem = plane, buf, send_sem, recv_sem
        self.rows = buf.shape[1]

    def part(self, half, piece):
        if piece is None:
            return pl.ds(half * (self.rows // 2), self.rows // 2)
        return pl.ds(half * (self.rows // 2) + piece * (self.rows // 4), self.rows // 4)

    def copy(self, half, kind, d, a, arriving):
        plane = self.plane
        dd = 0 if d == 1 else 1
        hop = -d if arriving else 0
        if kind == "F1":
            k, q, piece = dd, plane.slot(half, hop, 0), None
        elif kind == "F2":
            k, q, piece = 2 + dd, plane.slot(half, hop - d, 0), dd
        elif kind == "G1":
            k, q, piece = 4 + 2 * a + dd, plane.slot(half, a, hop), None
        else:
            k, q, piece = 12 + 2 * a + dd, plane.slot(half, a, hop - d), dd
        to = plane.slot(half, d, 0) if kind[0] == "F" else plane.slot(half, 0, d)
        where = self.buf.at[q, self.part(half, piece)]
        return pltpu.make_async_remote_copy(
            src_ref=where, dst_ref=where, send_sem=self.send_sem.at[0], recv_sem=self.recv_sem.at[half * 20 + k],
            device_id={"dp": to}, device_id_type=MESH,
        )

    def send(self, kind, a=0):
        for half in (0, 1):
            for d in DIRS:
                self.copy(half, kind, d, a, False).start()

    def wait(self, kind, a=0):
        for half in (0, 1):
            for d in DIRS:
                self.copy(half, kind, d, a, True).wait_recv()

    def round0(self):
        self.send("F1")
        self.send("G1", 0)

    def round1(self):
        self.wait("F1")
        self.send("F2")
        self.send("G1", 1)
        self.send("G1", 3)
        self.wait("G1", 0)
        self.send("G2", 0)
        return ((0, 0), (0, 1), (0, 3), (1, 0), (3, 0))

    def round2(self):
        self.wait("F2")
        self.send("G1", 2)
        self.wait("G1", 1)
        self.send("G2", 1)
        self.wait("G1", 3)
        self.send("G2", 3)
        self.wait("G2", 0)
        return ((1, 1), (1, 3), (3, 1), (3, 3), (2, 0), (0, 2))

    def round3(self):
        self.wait("G1", 2)
        self.send("G2", 2)
        self.wait("G2", 1)
        self.wait("G2", 3)
        return ((2, 1), (2, 3), (1, 2), (3, 2))

    def round4(self):
        self.wait("G2", 2)
        return ((2, 2),)

    def finish(self):
        whole = self.buf.at[pl.ds(0, GROUP - 1)]
        pltpu.make_async_remote_copy(
            src_ref=whole, dst_ref=whole, send_sem=self.send_sem.at[0], recv_sem=self.recv_sem.at[0],
            device_id={"dp": self.plane.slot(0, 1, 0)}, device_id_type=MESH,
        ).wait_send()


class Scatter:
    def __init__(self, plane, part, land, send_sem, recv_sem):
        self.plane, self.part, self.land = plane, part, land
        self.send_sem, self.recv_sem = send_sem, recv_sem
        self.quarter = part.shape[1] // 4

    def rows(self, half, piece):
        return pl.ds((2 * half + piece) * self.quarter, self.quarter)

    def index(self, half, kind, d, a):
        dd = 0 if d == 1 else 1
        base = {"S1": 0, "S2": 8, "S3": 16, "U1": 24, "U2": 26, "U3": 28}[kind]
        return half * 30 + base + (2 * a if kind[0] == "S" else 0) + dd

    def copy(self, half, kind, d, a):
        plane = self.plane
        dd = 0 if d == 1 else 1
        far = 2 if kind[1] == "1" else d
        piece = 1 - dd if kind[1] == "2" else dd
        if kind[0] == "S":
            q, to = plane.slot(half, a, far), plane.slot(half, 0, d)
        else:
            q, to = plane.slot(half, far, 0), plane.slot(half, d, 0)
        k = self.index(half, kind, d, a)
        return pltpu.make_async_remote_copy(
            src_ref=self.part.at[q, self.rows(half, piece)], dst_ref=self.land.at[k],
            send_sem=self.send_sem.at[0], recv_sem=self.recv_sem.at[k],
            device_id={"dp": to}, device_id_type=MESH,
        )

    def landed(self, half, kind, d, a=0):
        self.copy(half, kind, d, a).wait_recv()
        return self.land[self.index(half, kind, d, a)].astype(F32)

    def send_chunk(self, dz, dx):
        for half, a, far in ((0, dx, dz), (1, dz, dx)):
            if far == 2:
                for d in DIRS:
                    self.copy(half, "S1", d, a).start()
            elif far == 1:
                self.copy(half, "S2", 1, a).start()
            elif far == 3:
                self.copy(half, "S2", -1, a).start()

    def pass_on(self, a):
        for half in (0, 1):
            for d in DIRS:
                q, rows = self.plane.slot(half, a, d), self.rows(half, 0 if d == 1 else 1)
                total = self.part[q, rows].astype(F32) + self.landed(half, "S1", d, a)
                self.part[q, rows] = total.astype(BF16)
                self.copy(half, "S3", d, a).start()

    def settle(self, a):
        for half in (0, 1):
            q = self.plane.slot(half, a, 0)
            for piece, d in ((0, 1), (1, -1)):
                rows = self.rows(half, piece)
                total = self.part[q, rows].astype(F32) + self.landed(half, "S3", d, a) + self.landed(half, "S2", -d, a)
                self.part[q, rows] = total.astype(BF16)
            if a == 2:
                for d in DIRS:
                    self.copy(half, "U1", d, 0).start()
            elif a == 1:
                self.copy(half, "U2", 1, 0).start()
            elif a == 3:
                self.copy(half, "U2", -1, 0).start()

    def pass_last(self):
        for half in (0, 1):
            for d in DIRS:
                q, rows = self.plane.slot(half, d, 0), self.rows(half, 0 if d == 1 else 1)
                total = self.part[q, rows].astype(F32) + self.landed(half, "U1", d)
                self.part[q, rows] = total.astype(BF16)
                self.copy(half, "U3", d, 0).start()

    def result(self, total):
        me = self.plane.me
        for half in (0, 1):
            for piece, d in ((0, 1), (1, -1)):
                rows = self.rows(half, piece)
                total[rows] = (
                    self.part[me, rows].astype(F32) + self.landed(half, "U3", d) + self.landed(half, "U2", -d)
                )

    def finish(self):
        whole = self.part.at[pl.ds(0, GROUP - 1)]
        pltpu.make_async_remote_copy(
            src_ref=whole, dst_ref=whole, send_sem=self.send_sem.at[0], recv_sem=self.recv_sem.at[0],
            device_id={"dp": self.plane.slot(0, 1, 0)}, device_id_type=MESH,
        ).wait_send()


class Ring:
    def __init__(self, plane, buf, land, send_sem, recv_sem):
        self.plane, self.buf, self.land, self.send_sem, self.recv_sem = plane, buf, land, send_sem, recv_sem
        self.z = plane.place[1][0]
        self.half = buf.shape[1] // 2

    def piece(self, which):
        return pl.ds(which * self.half, self.half)

    def copy(self, src, dst, k, d):
        return pltpu.make_async_remote_copy(
            src_ref=src, dst_ref=dst, send_sem=self.send_sem.at[0], recv_sem=self.recv_sem.at[k],
            device_id={"dp": self.plane.slot(0, 0, d)}, device_id_type=MESH,
        )

    def gather_copy(self, kind, d, arriving):
        dd = 0 if d == 1 else 1
        hop = -d if arriving else 0
        if kind == 1:
            where = self.buf.at[wrap(self.z + hop)]
        else:
            where = self.buf.at[wrap(self.z + hop - d), self.piece(dd)]
        return self.copy(where, where, 2 * (kind - 1) + dd, d)

    def gather_send(self, kind):
        for d in DIRS:
            self.gather_copy(kind, d, False).start()

    def gather_wait(self, kind):
        for d in DIRS:
            self.gather_copy(kind, d, True).wait_recv()

    def sum_copy(self, kind, d):
        dd = 0 if d == 1 else 1
        far = 2 if kind == 1 else d
        k = 2 * (kind - 1) + dd
        src = self.buf.at[wrap(self.z + far), self.piece(1 - dd if kind == 2 else dd)]
        return self.copy(src, self.land.at[k], k, d)

    def landed(self, kind, d):
        self.sum_copy(kind, d).wait_recv()
        return self.land[2 * (kind - 1) + (0 if d == 1 else 1)].astype(F32)

    def sum_send(self):
        for kind in (1, 2):
            for d in DIRS:
                self.sum_copy(kind, d).start()

    def sum_pass(self):
        for d in DIRS:
            spot, rows = wrap(self.z + d), self.piece(0 if d == 1 else 1)
            self.buf[spot, rows] = (self.buf[spot, rows].astype(F32) + self.landed(1, d)).astype(BF16)
            self.sum_copy(3, d).start()

    def sum_result(self, total):
        for which, d in ((0, 1), (1, -1)):
            rows = self.piece(which)
            total[rows] = self.buf[self.z, rows].astype(F32) + self.landed(3, d) + self.landed(2, -d)

    def finish(self):
        whole = self.buf.at[pl.ds(0, RING - 1)]
        self.copy(whole, whole, 0, 1).wait_send()


class Exchange:
    def __init__(self, plane, sems):
        self.plane, self.sems = plane, sems

    def copy(self, src, dst, to):
        return pltpu.make_async_remote_copy(
            src_ref=src, dst_ref=dst, send_sem=self.sems.at[0], recv_sem=self.sems.at[1],
            device_id={"dp": to}, device_id_type=MESH,
        )

    def start(self, src, dst):
        for k in range(1, GROUP):
            to = lax.rem(self.plane.me + k, GROUP)
            self.copy(src(to), dst(k), to).start()

    def wait_recv(self, whole):
        self.copy(whole, whole, lax.rem(self.plane.me + 1, GROUP)).wait_recv()

    def wait_send(self, whole):
        self.copy(whole, whole, lax.rem(self.plane.me + 1, GROUP)).wait_send()


def whole_kernel(
    sections, scale_a, scale_b,
    h_hbm, top_hbm, w_hbm, m_hbm, v_hbm, list_ref, owner_ref,
    w_out, m_out, v_out, blocks_out, ids_out,
    h_v, w_v, wide, m_v, v_v,
    all_a, part_a, land_a, ring_b, slice_b, merged, u_part, u_land, u_turn, u_near, outs, grad_out, part_b, land_b,
    rows_a, cross_all, cross_part, cross_land, mixed_part, mixed_land, mixed,
    acc, out_n, u_all, u_acc, deltas, total, relayed, tiles, outbox, w_new, ids_in, ids_ref, slot_ref,
    local_sem, ga_send, ga_recv, gb_send, gb_recv, sa_send, sa_recv, sb_send, sb_recv,
    row_send, row_turn, row_recv, cross_send, cross_turn, cross_recv, u_send, u_turn_sem, u_recv, swap_sem, near_sem,
):
    s = lax.axis_index("section")
    plane = Plane()
    me = plane.me
    width = w_v.shape[0] // 2
    chunk = cross_part.shape[0] // GROUP
    rank = rows_a.shape[2]
    level, core = s // 2, lax.rem(s, 2)
    x = plane.place[0][0]
    tokens = h_v.shape[0]
    half_cols = pl.ds(pl.multiple_of(core * (width // 2), width // 2), width // 2)

    loads = [
        pltpu.make_async_copy(src, dst, local_sem.at[k])
        for k, (src, dst) in enumerate(((w_hbm, w_v), (h_hbm, h_v), (m_hbm, m_v), (v_hbm, v_v)))
    ]
    own_cols = pl.ds(pl.multiple_of((level * RING + x) * width, width), width)
    loads.append(pltpu.make_async_copy(top_hbm.at[:, own_cols], merged.at[x], local_sem.at[4]))
    for load in loads:
        load.start()

    barrier = pltpu.get_barrier_semaphore()
    for k in range(1, GROUP):
        pl.semaphore_signal(barrier, inc=1, device_id={"dp": lax.rem(me + k, GROUP)}, device_id_type=MESH)
    for k in range(1, sections):
        pl.semaphore_signal(barrier, inc=1, device_id={"section": lax.rem(s + k, sections)}, device_id_type=MESH)

    loads[0].wait()
    wide[...] = w_v[...].astype(F32)
    all_a[me] = wide[pl.ds(0, width, stride=2), :].astype(BF16)
    own_b = wide[pl.ds(1, width, stride=2), :]
    ring_b[plane.place[1][0]] = own_b.astype(BF16)
    pl.semaphore_wait(barrier, GROUP - 1 + sections - 1)

    gather_a = Gather(plane, all_a, ga_send, ga_recv)
    ring_gather = Ring(plane, ring_b, None, gb_send, gb_recv)
    scatter_a = Scatter(plane, part_a, land_a, sa_send, sa_recv)
    ring_sum = Ring(plane, part_b, land_b, sb_send, sb_recv)
    swap_cross = Exchange(plane, swap_sem.at[0])
    spread_cross = Exchange(plane, swap_sem.at[1])
    swap_mixed = Exchange(plane, swap_sem.at[2])
    spread_mixed = Exchange(plane, swap_sem.at[3])
    swap_ids = Exchange(plane, swap_sem.at[4])
    swap_tiles = Exchange(plane, swap_sem.at[5])

    def down(src, dst, send_sem, recv_sem, to):
        return pltpu.make_async_remote_copy(
            src_ref=src, dst_ref=dst, send_sem=send_sem, recv_sem=recv_sem,
            device_id={"section": to}, device_id_type=MESH,
        )

    def cross_copy(layer, sem, to):
        block = cross_all.at[layer, pl.ds((layer + 1) * rank, (sections - 1 - layer) * rank)]
        return down(block, block, sem, cross_recv.at[layer], to)

    def cross_outgoing(act):
        for layer in range(1, sections - 1):
            @pl.when(s == layer)
            def _():
                for to in range(layer // 2 - 1, -1, -1):
                    act(cross_copy(layer, cross_send.at[to], 2 * to + layer % 2))
                if layer % 2 == 1:
                    act(cross_copy(layer, cross_send.at[RING - 1], layer - 1))

    def cross_relay():
        for layer in range(sections - 2, 1, -1):
            @pl.when((layer // 2 > level) & (core == layer % 2))
            def _():
                cross_copy(layer, cross_turn.at[layer], s + 1 - 2 * core).wait_recv()
                cross_copy(layer, cross_turn.at[layer], s + 1 - 2 * core).start()

    def cross_rest():
        for layer in range(sections - 2, 0, -1):
            @pl.when((layer > s) & ((layer // 2 == level) | (core != layer % 2)))
            def _():
                cross_copy(layer, cross_turn.at[layer], s + 1 - 2 * core).wait_recv()

    def cross_finish():
        cross_outgoing(lambda copy: copy.wait_send())
        for layer in range(sections - 2, 1, -1):
            @pl.when((layer // 2 > level) & (core == layer % 2))
            def _():
                cross_copy(layer, cross_turn.at[layer], s + 1 - 2 * core).wait_send()

    class Cascade:
        def __init__(self, blocks, send_sem, turn_sem, recv_sem):
            self.blocks, self.send_sem, self.turn_sem, self.recv_sem = blocks, send_sem, turn_sem, recv_sem

        def copy(self, src, layer, sem, to):
            return down(src, self.blocks.at[layer], sem, self.recv_sem.at[layer], to)

        def outgoing(self, src, act):
            for to in range(sections // 2 - 2, -1, -1):
                @pl.when(to < level)
                def _():
                    act(self.copy(src, s, self.send_sem.at[to], 2 * to + core))

            @pl.when(core == 1)
            def _():
                act(self.copy(src, s, self.send_sem.at[RING - 1], s - 1))

        def send(self, src):
            self.outgoing(src, lambda copy: copy.start())

        def relay(self):
            for layer in range(sections - 1, 1, -1):
                @pl.when((layer // 2 > level) & (core == layer % 2))
                def _():
                    block = self.blocks.at[layer]
                    self.copy(block, layer, self.turn_sem.at[layer], s + 1 - 2 * core).wait_recv()
                    self.copy(block, layer, self.turn_sem.at[layer], s + 1 - 2 * core).start()

        def rest(self):
            for layer in range(sections - 1, 0, -1):
                @pl.when((layer > s) & ((layer // 2 == level) | (core != layer % 2)))
                def _():
                    block = self.blocks.at[layer]
                    self.copy(block, layer, self.turn_sem.at[layer], s + 1 - 2 * core).wait_recv()

        def finish(self, src):
            self.outgoing(src, lambda copy: copy.wait_send())
            for layer in range(sections - 1, 1, -1):
                @pl.when((layer // 2 > level) & (core == layer % 2))
                def _():
                    self.copy(self.blocks.at[layer], layer, self.turn_sem.at[layer], s + 1 - 2 * core).wait_send()

    row_cascade = Cascade(rows_a, row_send, row_turn, row_recv)
    u_cascade = Cascade(u_all, u_send, u_turn_sem, u_recv)

    def near(src, dst, group, k):
        to = plane.slot(0, k, 0)
        return pltpu.make_async_remote_copy(
            src_ref=src, dst_ref=dst, send_sem=near_sem.at[group, 0], recv_sem=near_sem.at[group, k],
            device_id={"dp": to}, device_id_type=MESH,
        )

    def across(src, dst, group, k):
        to = wrap(level + k) * 2 + core
        return pltpu.make_async_remote_copy(
            src_ref=src, dst_ref=dst, send_sem=near_sem.at[group, 0], recv_sem=near_sem.at[group, k],
            device_id={"section": to}, device_id_type=MESH,
        )

    def twin(src, dst, group, k):
        return pltpu.make_async_remote_copy(
            src_ref=src, dst_ref=dst, send_sem=near_sem.at[group, 0], recv_sem=near_sem.at[group, k],
            device_id={"section": s + 1 - 2 * core}, device_id_type=MESH,
        )

    HOPS = (1, 3, 2)

    def top_copy(k):
        cols = pl.ds(
            pl.multiple_of((level * RING + wrap(x + k)) * width + core * (width // 2), width // 2), width // 2
        )
        return near(top_hbm.at[:, cols], merged.at[x, :, half_cols], 0, k)

    ring_gather.gather_send(1)
    for k in HOPS:
        top_copy(k).start()
    gather_a.round0()
    row_cascade.send(all_a.at[me])

    entries = list_ref.shape[1]
    chosen = [list_ref[0, i] for i in range(entries)]
    owners = [owner_ref[0, i] for i in range(entries)]
    keys = []
    for i in range(entries):
        place = jnp.int32(0)
        for j in range(i):
            place += (owners[j] == owners[i]).astype(jnp.int32)
        keys.append(owners[i] * CAP + place)
    lane = lax.broadcasted_iota(jnp.int32, ids_ref.shape[1:], 1)

    def fill_slot(owner, carry):
        row = jnp.full(ids_ref.shape[1:], -1, jnp.int32)
        for place in range(CAP):
            index = jnp.int32(-1)
            for i in range(entries):
                index = jnp.where(keys[i] == owner * CAP + place, chosen[i], index)
            slot_ref[owner * CAP + place] = index
            row = jnp.where(lane == place, jnp.where(index >= 0, me * tiles.shape[0] + index, -1), row)
        ids_ref[owner] = row
        return carry

    lax.fori_loop(0, GROUP, fill_slot, 0)
    swap_ids.start(lambda q: ids_ref.at[q], lambda k: ids_in.at[me])
    ids_in[me] = ids_ref[me]
    for layer in range(sections):
        @pl.when(layer <= s)
        def _():
            rows_a[layer] = jnp.zeros(rows_a.shape[1:], BF16)
    own_bt = own_b.T.astype(BF16)

    ring_gather.gather_wait(1)
    ring_gather.gather_send(2)
    gather_a.round1()

    def passed_on(k):
        spot = merged.at[wrap(x - k), :, half_cols]
        return twin(spot, spot, 1, k)

    for k in HOPS:
        spot = merged.at[wrap(x - k), :, half_cols]
        near(spot, spot, 0, k).wait_recv()
        passed_on(k).start()
    ring_gather.gather_wait(2)
    for k in HOPS:
        across(ring_b.at[wrap(level + k)], slice_b.at[level], 2, k).start()
    slice_b[level] = ring_b[level]

    row_cascade.relay()
    row_cascade.rest()
    for layer in range(sections):
        cross_part[layer * rank:(layer + 1) * rank] = jnp.dot(
            own_bt, rows_a[layer], preferred_element_type=F32
        ).astype(BF16)

    def piece(ref, q):
        return ref.at[pl.ds(pl.multiple_of(q * chunk, chunk), chunk)]

    swap_cross.start(lambda q: piece(cross_part, q), lambda k: cross_land.at[k - 1])
    gather_a.round2()

    loads[4].wait()
    other_cols = pl.ds(pl.multiple_of((1 - core) * (width // 2), width // 2), width // 2)
    for k in HOPS:
        spot = merged.at[wrap(x - k), :, other_cols]
        twin(spot, spot, 1, k).wait_recv()

    def direct(layer_level, dst):
        for spot in range(RING):
            dst[spot] = jnp.dot(merged[spot], slice_b[layer_level], preferred_element_type=F32).astype(BF16)

    for n, k in enumerate(HOPS):
        across(slice_b.at[wrap(level - k)], slice_b.at[wrap(level - k)], 2, k).wait_recv()
        direct(wrap(level - k), u_part.at[n])
        across(u_part.at[n], u_land.at[n], 3, RING - k).start()
    direct(level, u_part.at[RING - 1])
    gather_a.round3()

    swap_cross.wait_recv(cross_land)
    own_rows = pl.ds(pl.multiple_of(me * chunk, chunk), chunk)
    cross_sum = cross_part[own_rows].astype(F32)
    for k in range(GROUP - 1):
        cross_sum = cross_sum + cross_land[k].astype(F32)
    cross_all[s, own_rows] = (cross_sum * (scale_a * scale_b)).astype(BF16)
    spread_cross.start(lambda q: cross_all.at[s, own_rows], lambda k: cross_all.at[s, own_rows])

    gather_a.round4()
    loads[1].wait()

    def forward(left, blocks, q):
        cols = pl.ds(pl.multiple_of(q * width, width), width)
        return jnp.dot(left[:, cols], blocks[q], preferred_element_type=F32)

    acc[...] = jnp.zeros_like(acc)

    def forward_a(q, carry):
        acc[...] += forward(h_v, all_a, q)
        return carry

    lax.fori_loop(0, GROUP // 2, forward_a, 0)

    spread_cross.wait_recv(cross_all.at[s, pl.ds(0, (GROUP - 1) * chunk)])
    cross_outgoing(lambda copy: copy.start())

    for n, k in enumerate(HOPS):
        across(u_part.at[n], u_land.at[n], 3, RING - k).wait_recv()

    def turn(spot):
        summed = u_part[RING - 1, spot].astype(F32)
        for n in range(RING - 1):
            summed = summed + u_land[n, spot].astype(F32)
        return summed

    def u_copy(k):
        return near(u_turn.at[k - 1], u_near.at[k - 1], 4, k)

    for k in HOPS:
        u_turn[k - 1] = turn(wrap(x + k)).astype(BF16)
        u_copy(k).start()
    lax.fori_loop(GROUP // 2, GROUP, forward_a, 0)
    adapter_out = acc[...] * scale_a
    out_n[...] = adapter_out.astype(BF16)
    outs[level, x] = adapter_out.T.astype(BF16)
    for k in HOPS:
        near(outs.at[level, x], outs.at[level, x], 5, k).start()


    def backward(left, right, part, q):
        cols = pl.ds(pl.multiple_of(q * width, width), width)
        part[q] = jnp.dot(left, right[:, cols], preferred_element_type=F32).astype(BF16)

    order = [(2, 2)] + [(2, k) for k in (0, 1, 3)] + [(k, 2) for k in (0, 1, 3)]
    order += [(1, 1), (1, 3), (3, 1), (3, 3), (1, 0), (3, 0), (0, 1), (0, 3), (0, 0)]
    own_direct = turn(x)
    for k in HOPS:
        u_copy(k).wait_recv()
        own_direct = own_direct + u_near[k - 1].astype(F32)

    u_all[s] = (own_direct * scale_b).T.astype(BF16)
    u_cascade.send(u_all.at[s])
    for k in HOPS:
        spot = outs.at[level, wrap(x - k)]
        near(spot, spot, 5, k).wait_recv()
    for k in HOPS:
        across(outs.at[level], outs.at[level], 6, k).start()
    cross_relay()
    cross_rest()
    u_cascade.relay()
    u_cascade.rest()
    for layer in range(sections):
        @pl.when(layer >= s)
        def _():
            u_acc[layer] = u_all[layer].astype(F32)
    for layer in range(sections - 1, -1, -1):
        @pl.when(layer >= s)
        def _():
            delta = u_acc[layer].astype(BF16)
            deltas[layer] = delta
            for lower in range(layer):
                @pl.when(lower >= s)
                def _():
                    u_acc[lower] += jnp.dot(
                        cross_all[lower, layer * rank:(layer + 1) * rank], delta, preferred_element_type=F32
                    )

    for layer in range(sections):
        @pl.when(layer > s)
        def _():
            mixed_part[layer * rank:(layer + 1) * rank] = jnp.dot(
                deltas[layer], out_n[...], preferred_element_type=F32
            ).astype(BF16)

        @pl.when(layer <= s)
        def _():
            mixed_part[layer * rank:(layer + 1) * rank] = jnp.zeros((rank, rank), BF16)
    swap_mixed.start(lambda q: piece(mixed_part, q), lambda k: mixed_land.at[k - 1])

    for dz, dx in order[:7]:
        backward(deltas[s], h_v, part_a, plane.away(dz, dx))
        scatter_a.send_chunk(dz, dx)

    def top_grad_of(layer_level):
        summed = jnp.dot(outs[layer_level, 0], merged[0], preferred_element_type=F32)
        for spot in range(1, RING):
            summed = summed + jnp.dot(outs[layer_level, spot], merged[spot], preferred_element_type=F32)
        return summed.astype(BF16)

    for n, k in enumerate(HOPS):
        spot = outs.at[wrap(level - k)]
        across(spot, spot, 6, k).wait_recv()
        grad_out[n] = top_grad_of(wrap(level - k))
        across(grad_out.at[n], part_b.at[level], 7, RING - k).start()
    part_b[level] = top_grad_of(level)
    for dz, dx in order[7:]:
        backward(deltas[s], h_v, part_a, plane.away(dz, dx))
        scatter_a.send_chunk(dz, dx)

    swap_mixed.wait_recv(mixed_land)
    mixed_sum = mixed_part[own_rows].astype(F32)
    for k in range(GROUP - 1):
        mixed_sum = mixed_sum + mixed_land[k].astype(F32)
    mixed[own_rows] = mixed_sum.astype(BF16)
    spread_mixed.start(lambda q: mixed.at[own_rows], lambda k: mixed.at[own_rows])
    for a in (2, 1, 3, 0):
        scatter_a.pass_on(a)
    for k in HOPS:
        spot = part_b.at[wrap(level - k)]
        across(spot, spot, 7, k).wait_recv()
    ring_sum.sum_send()
    for a in (2, 1, 3, 0):
        scatter_a.settle(a)
    ring_sum.sum_pass()
    scatter_a.pass_last()
    spread_mixed.wait_recv(mixed.at[pl.ds(0, (GROUP - 1) * chunk)])
    loads[2].wait()
    loads[3].wait()

    def adam(which, gradient_of):
        for block in range(width // BS):
            rows = pl.ds(2 * BS * block + which, BS, stride=2)
            gradient = gradient_of(pl.ds(block * BS, BS))
            new_first = beta_one * m_v[rows, :] + (1.0 - beta_one) * gradient
            new_second = beta_two * v_v[rows, :] + (1.0 - beta_two) * gradient * gradient
            master = wide[rows, :]
            update = new_first / correct_one / (jnp.sqrt(new_second / correct_two) + adam_eps)
            fresh = master - learn_rate * (update + decay_rate * master)
            m_v[rows, :] = new_first
            v_v[rows, :] = new_second
            wide[rows, :] = fresh
            tiles[2 * block + which] = fresh.astype(BF16)

    relayed[...] = jnp.dot(rows_a[0], mixed[0:rank], preferred_element_type=F32)
    for layer in range(1, sections):
        relayed[...] += jnp.dot(
            rows_a[layer], mixed[layer * rank:(layer + 1) * rank], preferred_element_type=F32
        )
    ring_sum.sum_result(total)
    adam(1, lambda rows: (total[:, rows].T + relayed[rows] * scale_a) * scale_b)

    scatter_a.result(total)
    adam(0, lambda rows: total[:, rows].T * scale_a)

    for k in range(1, GROUP + 1):
        owner = lax.rem(me + k, GROUP)
        for place in range(CAP):
            index = slot_ref[owner * CAP + place]
            tile = tiles[jnp.maximum(index, 0)]
            outbox[owner, place] = jnp.where(index >= 0, tile, jnp.zeros_like(tile))
        if k < GROUP:
            swap_tiles.copy(outbox.at[owner], blocks_out.at[me], owner).start()
    kept = pltpu.make_async_copy(outbox.at[me], blocks_out.at[me], local_sem.at[5])
    kept.start()
    w_new[...] = wide[...].astype(BF16)
    stores = [
        pltpu.make_async_copy(src, dst, local_sem.at[k])
        for k, (src, dst) in enumerate(((w_new, w_out), (m_v, m_out), (v_v, v_out)))
    ]
    for store in stores:
        store.start()
    swap_ids.wait_recv(ids_in.at[pl.ds(0, GROUP - 1)])
    stores.append(pltpu.make_async_copy(ids_in, ids_out, local_sem.at[3]))
    stores[-1].start()

    gather_a.finish()
    ring_gather.finish()
    scatter_a.finish()
    ring_sum.finish()
    for group, whole in (
        (0, merged.at[pl.ds(0, RING - 1), :, half_cols]), (1, merged.at[pl.ds(0, RING - 1), :, half_cols]),
        (2, slice_b.at[pl.ds(0, RING - 1)]), (3, u_land), (4, u_near),
        (5, outs.at[0, pl.ds(0, RING - 1)]), (6, outs.at[pl.ds(0, RING - 1)]), (7, grad_out),
    ):
        near(whole, whole, group, 1).wait_send()
    row_cascade.finish(all_a.at[me])
    cross_finish()
    u_cascade.finish(u_all.at[s])
    swap_ids.wait_send(ids_ref.at[pl.ds(0, GROUP - 1)])
    swap_cross.wait_send(cross_land)
    swap_mixed.wait_send(mixed_land)
    spread_cross.wait_send(mixed.at[pl.ds(0, (GROUP - 1) * chunk)])
    spread_mixed.wait_send(mixed.at[pl.ds(0, (GROUP - 1) * chunk)])
    swap_tiles.wait_send(outbox.at[pl.ds(0, GROUP - 1)])
    swap_tiles.wait_recv(blocks_out.at[pl.ds(0, GROUP - 1)])
    kept.wait()
    for store in stores:
        store.wait()


def hand_over(
    w_in, m_in, v_in, blocks_in, ids_in, w_out, m_out, v_out, blocks_out, ids_out, w_v, m_v, v_v, blocks_v, in_sem, out_sem
):
    arrays = ((m_in, m_v, m_out), (v_in, v_v, v_out), (blocks_in, blocks_v, blocks_out), (w_in, w_v, w_out))
    fetches, stores = [], []
    for array, (src, stage, dst) in enumerate(arrays):
        half = src.shape[0] // 2
        for k in range(2):
            part = pl.ds(k * half, half)
            fetches.append(pltpu.make_async_copy(src.at[part], stage.at[part], in_sem.at[2 * array + k]))
            stores.append(pltpu.make_async_copy(stage.at[part], dst.at[part], out_sem.at[2 * array + k]))
    for fetch in fetches:
        fetch.start()
    ids_out[...] = ids_in[:, 0, :].T[:CAP, :]
    for fetch, store in zip(fetches, stores):
        fetch.wait()
        store.start()
    for store in stores:
        store.wait()


def shards(section_inputs, top_grad, weights, first_moment, second_moment, block_list, block_owner):
    sections = lax.axis_size("section")
    model_width = section_inputs.shape[3]
    rank = weights.shape[3]
    width = weights.shape[1]
    tokens = section_inputs.shape[1] * section_inputs.shape[2]
    chunk = sections * rank // GROUP
    entries = block_list.shape[2]
    scale_a = model_width ** (-0.5)
    scale_b = rank ** (-0.5)

    any_spec = pl.BlockSpec(memory_space=pl.ANY)
    vmem = pl.BlockSpec(memory_space=pltpu.VMEM)
    dma = pltpu.SemaphoreType.DMA
    new_weights, new_first, new_second, blocks, got_ids = pl.pallas_call(
        functools.partial(whole_kernel, sections, scale_a, scale_b),
        out_shape=(
            jax.ShapeDtypeStruct((2 * width, rank), BF16),
            jax.ShapeDtypeStruct((2 * width, rank), F32),
            jax.ShapeDtypeStruct((2 * width, rank), F32),
            jax.ShapeDtypeStruct((GROUP, CAP, BS, BS), BF16),
            jax.ShapeDtypeStruct((GROUP, 8, 128), jnp.int32),
        ),
        in_specs=[any_spec] * 5 + [pl.BlockSpec(memory_space=pltpu.SMEM)] * 2,
        out_specs=(any_spec,) * 5,
        scratch_shapes=[
            pltpu.VMEM((tokens, model_width), BF16),
            pltpu.VMEM((2 * width, rank), BF16),
            pltpu.VMEM((2 * width, rank), F32),
            pltpu.VMEM((2 * width, rank), F32),
            pltpu.VMEM((2 * width, rank), F32),
            pltpu.VMEM((GROUP, width, rank), BF16),
            pltpu.VMEM((GROUP, rank, width), BF16),
            pltpu.VMEM((60, rank // 4, width), BF16),
            pltpu.VMEM((RING, width, rank), BF16),
            pltpu.VMEM((RING, width, rank), BF16),
            pltpu.VMEM((RING, tokens, width), BF16),
            pltpu.VMEM((RING, RING, tokens, rank), BF16),
            pltpu.VMEM((RING - 1, RING, tokens, rank), BF16),
            pltpu.VMEM((RING - 1, tokens, rank), BF16),
            pltpu.VMEM((RING - 1, tokens, rank), BF16),
            pltpu.VMEM((RING, RING, rank, tokens), BF16),
            pltpu.VMEM((RING - 1, rank, width), BF16),
            pltpu.VMEM((RING, rank, width), BF16),
            pltpu.VMEM((6, rank // 2, width), BF16),
            pltpu.VMEM((sections, width, rank), BF16),
            pltpu.VMEM((sections, sections * rank, rank), BF16),
            pltpu.VMEM((sections * rank, rank), BF16),
            pltpu.VMEM((GROUP - 1, chunk, rank), BF16),
            pltpu.VMEM((sections * rank, rank), BF16),
            pltpu.VMEM((GROUP - 1, chunk, rank), BF16),
            pltpu.VMEM((sections * rank, rank), BF16),
            pltpu.VMEM((tokens, rank), F32),
            pltpu.VMEM((tokens, rank), BF16),
            pltpu.VMEM((sections, rank, tokens), BF16),
            pltpu.VMEM((sections, rank, tokens), F32),
            pltpu.VMEM((sections, rank, tokens), BF16),
            pltpu.VMEM((rank, width), F32),
            pltpu.VMEM((width, rank), F32),
            pltpu.VMEM((2 * width // BS, BS, BS), BF16),
            pltpu.VMEM((GROUP, CAP, BS, BS), BF16),
            pltpu.VMEM((2 * width, rank), BF16),
            pltpu.VMEM((GROUP, 8, 128), jnp.int32),
            pltpu.VMEM((GROUP, 8, 128), jnp.int32),
            pltpu.SMEM((GROUP * CAP,), jnp.int32),
            dma((6,)),
            dma((1,)), dma((40,)), dma((1,)), dma((4,)),
            dma((1,)), dma((60,)), dma((1,)), dma((6,)),
            dma((RING,)), dma((sections,)), dma((sections,)),
            dma((RING,)), dma((sections,)), dma((sections,)),
            dma((RING,)), dma((sections,)), dma((sections,)),
            dma((6, 2)), dma((8, RING)),
        ],
        compiler_params=pltpu.CompilerParams(
            collective_id=0, has_side_effects=True, vmem_limit_bytes=62 * 1024 * 1024
        ),
        cost_estimate=pl.CostEstimate(
            flops=8 * tokens * model_width * rank, bytes_accessed=4 * tokens * model_width, transcendentals=0
        ),
    )(
        section_inputs.reshape(tokens, model_width),
        top_grad.reshape(tokens, model_width),
        weights.reshape(2 * width, rank),
        first_moment.reshape(2 * width, rank),
        second_moment.reshape(2 * width, rank),
        block_list.reshape(1, entries),
        block_owner.reshape(1, entries),
    )
    results = (new_weights, new_first, new_second, blocks)
    *results, got_ids = pl.pallas_call(
        hand_over,
        out_shape=(
            *(jax.ShapeDtypeStruct(array.shape, array.dtype) for array in results),
            jax.ShapeDtypeStruct((CAP, GROUP), jnp.int32),
        ),
        in_specs=[any_spec] * 4 + [vmem],
        out_specs=(any_spec,) * 4 + (vmem,),
        scratch_shapes=[pltpu.VMEM(array.shape, array.dtype) for array in results] + [dma((8,)), dma((8,))],
    )(*results, got_ids)
    new_weights, new_first, new_second, blocks = results
    return (
        new_weights.reshape(weights.shape),
        new_first.reshape(weights.shape),
        new_second.reshape(weights.shape),
        blocks[None, None],
        got_ids.T[None, None],
    )


def solution(mesh):
    placed = (
        P("section", None, "dp", None),
        P(None, "dp", None),
        P("section", "dp", None, None),
        P("section", "dp", None, None),
        P("section", "dp", None, None),
        P("section", "dp", None),
        P("section", "dp", None, None),
    )
    return jax.shard_map(
        shards,
        mesh=mesh,
        in_specs=placed,
        out_specs=(
            P("section", "dp", None, None),
            P("section", "dp", None, None),
            P("section", "dp", None, None),
            P("section", "dp", None, None, None, None),
            P("section", "dp", None, None),
        ),
        check_vma=False,
    )
```

```python
import functools

import jax
import jax.numpy as jnp
from jax import lax
from jax.experimental import pallas as pl
from jax.experimental.pallas import tpu as pltpu
from jax.sharding import PartitionSpec as P

BS = 128
CAP = 2
RING = 4
GROUP = RING * RING

beta_one = 0.9
beta_two = 0.999
correct_one = 1.0 - 0.9**10
correct_two = 1.0 - 0.999**10
learn_rate = 0.01
decay_rate = 0.1
adam_eps = 1e-08

MESH = pl.DeviceIdType.MESH
F32 = jnp.float32
BF16 = jnp.bfloat16
DIRS = (1, -1)
SHIFTS = (0, 1, 3, 2)


def wrap(value):
    return lax.rem(value + 2 * RING, RING)


class Plane:
    def __init__(self):
        me = lax.axis_index("dp")
        self.me = me
        z, x = me // RING, lax.rem(me, RING)
        self.place = ((x, z), (z, x))

    def slot(self, half, first, second):
        i, j = self.place[half]
        i, j = wrap(i + first), wrap(j + second)
        return j * RING + i if half == 0 else i * RING + j

    def away(self, dz, dx):
        return self.slot(1, dz, dx)


class Gather:
    def __init__(self, plane, buf, send_sem, recv_sem):
        self.plane, self.buf, self.send_sem, self.recv_sem = plane, buf, send_sem, recv_sem
        self.rows = buf.shape[1]

    def part(self, half, piece):
        if piece is None:
            return pl.ds(half * (self.rows // 2), self.rows // 2)
        return pl.ds(half * (self.rows // 2) + piece * (self.rows // 4), self.rows // 4)

    def copy(self, half, kind, d, a, arriving):
        plane = self.plane
        dd = 0 if d == 1 else 1
        hop = -d if arriving else 0
        if kind == "F1":
            k, q, piece = dd, plane.slot(half, hop, 0), None
        elif kind == "F2":
            k, q, piece = 2 + dd, plane.slot(half, hop - d, 0), dd
        elif kind == "G1":
            k, q, piece = 4 + 2 * a + dd, plane.slot(half, a, hop), None
        else:
            k, q, piece = 12 + 2 * a + dd, plane.slot(half, a, hop - d), dd
        to = plane.slot(half, d, 0) if kind[0] == "F" else plane.slot(half, 0, d)
        where = self.buf.at[q, self.part(half, piece)]
        return pltpu.make_async_remote_copy(
            src_ref=where, dst_ref=where, send_sem=self.send_sem.at[0], recv_sem=self.recv_sem.at[half * 20 + k],
            device_id={"dp": to}, device_id_type=MESH,
        )

    def send(self, kind, a=0):
        for half in (0, 1):
            for d in DIRS:
                self.copy(half, kind, d, a, False).start()

    def wait(self, kind, a=0):
        for half in (0, 1):
            for d in DIRS:
                self.copy(half, kind, d, a, True).wait_recv()

    def round0(self):
        self.send("F1")
        self.send("G1", 0)

    def round1(self):
        self.wait("F1")
        self.send("F2")
        self.send("G1", 1)
        self.send("G1", 3)
        self.wait("G1", 0)
        self.send("G2", 0)
        return ((0, 0), (0, 1), (0, 3), (1, 0), (3, 0))

    def round2(self):
        self.wait("F2")
        self.send("G1", 2)
        self.wait("G1", 1)
        self.send("G2", 1)
        self.wait("G1", 3)
        self.send("G2", 3)
        self.wait("G2", 0)
        return ((1, 1), (1, 3), (3, 1), (3, 3), (2, 0), (0, 2))

    def round3(self):
        self.wait("G1", 2)
        self.send("G2", 2)
        self.wait("G2", 1)
        self.wait("G2", 3)
        return ((2, 1), (2, 3), (1, 2), (3, 2))

    def round4(self):
        self.wait("G2", 2)
        return ((2, 2),)

    def finish(self):
        whole = self.buf.at[pl.ds(0, GROUP - 1)]
        pltpu.make_async_remote_copy(
            src_ref=whole, dst_ref=whole, send_sem=self.send_sem.at[0], recv_sem=self.recv_sem.at[0],
            device_id={"dp": self.plane.slot(0, 1, 0)}, device_id_type=MESH,
        ).wait_send()


class Scatter:
    def __init__(self, plane, part, land, send_sem, recv_sem):
        self.plane, self.part, self.land = plane, part, land
        self.send_sem, self.recv_sem = send_sem, recv_sem
        self.quarter = part.shape[1] // 4

    def rows(self, half, piece):
        return pl.ds((2 * half + piece) * self.quarter, self.quarter)

    def index(self, half, kind, d, a):
        dd = 0 if d == 1 else 1
        base = {"S1": 0, "S2": 8, "S3": 16, "U1": 24, "U2": 26, "U3": 28}[kind]
        return half * 30 + base + (2 * a if kind[0] == "S" else 0) + dd

    def copy(self, half, kind, d, a):
        plane = self.plane
        dd = 0 if d == 1 else 1
        far = 2 if kind[1] == "1" else d
        piece = 1 - dd if kind[1] == "2" else dd
        if kind[0] == "S":
            q, to = plane.slot(half, a, far), plane.slot(half, 0, d)
        else:
            q, to = plane.slot(half, far, 0), plane.slot(half, d, 0)
        k = self.index(half, kind, d, a)
        return pltpu.make_async_remote_copy(
            src_ref=self.part.at[q, self.rows(half, piece)], dst_ref=self.land.at[k],
            send_sem=self.send_sem.at[0], recv_sem=self.recv_sem.at[k],
            device_id={"dp": to}, device_id_type=MESH,
        )

    def landed(self, half, kind, d, a=0):
        self.copy(half, kind, d, a).wait_recv()
        return self.land[self.index(half, kind, d, a)].astype(F32)

    def send_chunk(self, dz, dx):
        for half, a, far in ((0, dx, dz), (1, dz, dx)):
            if far == 2:
                for d in DIRS:
                    self.copy(half, "S1", d, a).start()
            elif far == 1:
                self.copy(half, "S2", 1, a).start()
            elif far == 3:
                self.copy(half, "S2", -1, a).start()

    def pass_on(self, a):
        for half in (0, 1):
            for d in DIRS:
                q, rows = self.plane.slot(half, a, d), self.rows(half, 0 if d == 1 else 1)
                total = self.part[q, rows].astype(F32) + self.landed(half, "S1", d, a)
                self.part[q, rows] = total.astype(BF16)
                self.copy(half, "S3", d, a).start()

    def settle(self, a):
        for half in (0, 1):
            q = self.plane.slot(half, a, 0)
            for piece, d in ((0, 1), (1, -1)):
                rows = self.rows(half, piece)
                total = self.part[q, rows].astype(F32) + self.landed(half, "S3", d, a) + self.landed(half, "S2", -d, a)
                self.part[q, rows] = total.astype(BF16)
            if a == 2:
                for d in DIRS:
                    self.copy(half, "U1", d, 0).start()
            elif a == 1:
                self.copy(half, "U2", 1, 0).start()
            elif a == 3:
                self.copy(half, "U2", -1, 0).start()

    def pass_last(self):
        for half in (0, 1):
            for d in DIRS:
                q, rows = self.plane.slot(half, d, 0), self.rows(half, 0 if d == 1 else 1)
                total = self.part[q, rows].astype(F32) + self.landed(half, "U1", d)
                self.part[q, rows] = total.astype(BF16)
                self.copy(half, "U3", d, 0).start()

    def result(self, total):
        me = self.plane.me
        for half in (0, 1):
            for piece, d in ((0, 1), (1, -1)):
                rows = self.rows(half, piece)
                total[rows] = (
                    self.part[me, rows].astype(F32) + self.landed(half, "U3", d) + self.landed(half, "U2", -d)
                )

    def finish(self):
        whole = self.part.at[pl.ds(0, GROUP - 1)]
        pltpu.make_async_remote_copy(
            src_ref=whole, dst_ref=whole, send_sem=self.send_sem.at[0], recv_sem=self.recv_sem.at[0],
            device_id={"dp": self.plane.slot(0, 1, 0)}, device_id_type=MESH,
        ).wait_send()


class Ring:
    def __init__(self, plane, buf, land, send_sem, recv_sem):
        self.plane, self.buf, self.land, self.send_sem, self.recv_sem = plane, buf, land, send_sem, recv_sem
        self.z = plane.place[1][0]
        self.half = buf.shape[1] // 2

    def piece(self, which):
        return pl.ds(which * self.half, self.half)

    def copy(self, src, dst, k, d):
        return pltpu.make_async_remote_copy(
            src_ref=src, dst_ref=dst, send_sem=self.send_sem.at[0], recv_sem=self.recv_sem.at[k],
            device_id={"dp": self.plane.slot(0, 0, d)}, device_id_type=MESH,
        )

    def gather_copy(self, kind, d, arriving):
        dd = 0 if d == 1 else 1
        hop = -d if arriving else 0
        if kind == 1:
            where = self.buf.at[wrap(self.z + hop)]
        else:
            where = self.buf.at[wrap(self.z + hop - d), self.piece(dd)]
        return self.copy(where, where, 2 * (kind - 1) + dd, d)

    def gather_send(self, kind):
        for d in DIRS:
            self.gather_copy(kind, d, False).start()

    def gather_wait(self, kind):
        for d in DIRS:
            self.gather_copy(kind, d, True).wait_recv()

    def sum_copy(self, kind, d):
        dd = 0 if d == 1 else 1
        far = 2 if kind == 1 else d
        k = 2 * (kind - 1) + dd
        src = self.buf.at[wrap(self.z + far), self.piece(1 - dd if kind == 2 else dd)]
        return self.copy(src, self.land.at[k], k, d)

    def landed(self, kind, d):
        self.sum_copy(kind, d).wait_recv()
        return self.land[2 * (kind - 1) + (0 if d == 1 else 1)].astype(F32)

    def sum_send(self):
        for kind in (1, 2):
            for d in DIRS:
                self.sum_copy(kind, d).start()

    def sum_pass(self):
        for d in DIRS:
            spot, rows = wrap(self.z + d), self.piece(0 if d == 1 else 1)
            self.buf[spot, rows] = (self.buf[spot, rows].astype(F32) + self.landed(1, d)).astype(BF16)
            self.sum_copy(3, d).start()

    def sum_result(self, total):
        for which, d in ((0, 1), (1, -1)):
            rows = self.piece(which)
            total[rows] = self.buf[self.z, rows].astype(F32) + self.landed(3, d) + self.landed(2, -d)

    def finish(self):
        whole = self.buf.at[pl.ds(0, RING - 1)]
        self.copy(whole, whole, 0, 1).wait_send()


class Exchange:
    def __init__(self, plane, sems):
        self.plane, self.sems = plane, sems

    def copy(self, src, dst, to):
        return pltpu.make_async_remote_copy(
            src_ref=src, dst_ref=dst, send_sem=self.sems.at[0], recv_sem=self.sems.at[1],
            device_id={"dp": to}, device_id_type=MESH,
        )

    def start(self, src, dst):
        for k in range(1, GROUP):
            to = lax.rem(self.plane.me + k, GROUP)
            self.copy(src(to), dst(k), to).start()

    def wait_recv(self, whole):
        self.copy(whole, whole, lax.rem(self.plane.me + 1, GROUP)).wait_recv()

    def wait_send(self, whole):
        self.copy(whole, whole, lax.rem(self.plane.me + 1, GROUP)).wait_send()


def whole_kernel(
    sections, scale_a, scale_b,
    h_hbm, top_hbm, w_hbm, m_hbm, v_hbm, list_ref, owner_ref,
    w_out, m_out, v_out, blocks_out, ids_out,
    h_v, w_v, wide, m_v, v_v,
    all_a, part_a, land_a, ring_b, slice_b, merged, u_part, u_land, u_turn, u_near, outs, grad_out, part_b, land_b,
    rows_a, cross_all, cross_part, cross_land, mixed_part, mixed_land, mixed,
    acc, out_n, u_all, u_acc, deltas, total, relayed, tiles, outbox, w_new, ids_in, ids_ref, slot_ref,
    local_sem, ga_send, ga_recv, gb_send, gb_recv, sa_send, sa_recv, sb_send, sb_recv,
    row_send, row_turn, row_recv, cross_send, cross_turn, cross_recv, u_send, u_turn_sem, u_recv, swap_sem, near_sem,
):
    s = lax.axis_index("section")
    plane = Plane()
    me = plane.me
    width = w_v.shape[0] // 2
    chunk = cross_part.shape[0] // GROUP
    rank = rows_a.shape[2]
    level, core = s // 2, lax.rem(s, 2)
    x = plane.place[0][0]
    tokens = h_v.shape[0]
    half_cols = pl.ds(pl.multiple_of(core * (width // 2), width // 2), width // 2)

    loads = [
        pltpu.make_async_copy(src, dst, local_sem.at[k])
        for k, (src, dst) in enumerate(((w_hbm, w_v), (h_hbm, h_v), (m_hbm, m_v), (v_hbm, v_v)))
    ]
    own_cols = pl.ds(pl.multiple_of((level * RING + x) * width, width), width)
    loads.append(pltpu.make_async_copy(top_hbm.at[:, own_cols], merged.at[x], local_sem.at[4]))
    for load in loads:
        load.start()

    barrier = pltpu.get_barrier_semaphore()
    for k in range(1, GROUP):
        pl.semaphore_signal(barrier, inc=1, device_id={"dp": lax.rem(me + k, GROUP)}, device_id_type=MESH)
    for k in range(1, sections):
        pl.semaphore_signal(barrier, inc=1, device_id={"section": lax.rem(s + k, sections)}, device_id_type=MESH)

    loads[0].wait()
    wide[...] = w_v[...].astype(F32)
    all_a[me] = wide[pl.ds(0, width, stride=2), :].astype(BF16)
    own_b = wide[pl.ds(1, width, stride=2), :]
    ring_b[plane.place[1][0]] = own_b.astype(BF16)
    pl.semaphore_wait(barrier, GROUP - 1 + sections - 1)

    gather_a = Gather(plane, all_a, ga_send, ga_recv)
    ring_gather = Ring(plane, ring_b, None, gb_send, gb_recv)
    scatter_a = Scatter(plane, part_a, land_a, sa_send, sa_recv)
    ring_sum = Ring(plane, part_b, land_b, sb_send, sb_recv)
    swap_cross = Exchange(plane, swap_sem.at[0])
    spread_cross = Exchange(plane, swap_sem.at[1])
    swap_mixed = Exchange(plane, swap_sem.at[2])
    spread_mixed = Exchange(plane, swap_sem.at[3])
    swap_ids = Exchange(plane, swap_sem.at[4])
    swap_tiles = Exchange(plane, swap_sem.at[5])

    def down(src, dst, send_sem, recv_sem, to):
        return pltpu.make_async_remote_copy(
            src_ref=src, dst_ref=dst, send_sem=send_sem, recv_sem=recv_sem,
            device_id={"section": to}, device_id_type=MESH,
        )

    def cross_copy(layer, sem, to):
        block = cross_all.at[layer, pl.ds((layer + 1) * rank, (sections - 1 - layer) * rank)]
        return down(block, block, sem, cross_recv.at[layer], to)

    def cross_outgoing(act):
        for layer in range(1, sections - 1):
            @pl.when(s == layer)
            def _():
                for to in range(layer // 2 - 1, -1, -1):
                    act(cross_copy(layer, cross_send.at[to], 2 * to + layer % 2))
                if layer % 2 == 1:
                    act(cross_copy(layer, cross_send.at[RING - 1], layer - 1))

    def cross_relay():
        for layer in range(sections - 2, 1, -1):
            @pl.when((layer // 2 > level) & (core == layer % 2))
            def _():
                cross_copy(layer, cross_turn.at[layer], s + 1 - 2 * core).wait_recv()
                cross_copy(layer, cross_turn.at[layer], s + 1 - 2 * core).start()

    def cross_rest():
        for layer in range(sections - 2, 0, -1):
            @pl.when((layer > s) & ((layer // 2 == level) | (core != layer % 2)))
            def _():
                cross_copy(layer, cross_turn.at[layer], s + 1 - 2 * core).wait_recv()

    def cross_finish():
        cross_outgoing(lambda copy: copy.wait_send())
        for layer in range(sections - 2, 1, -1):
            @pl.when((layer // 2 > level) & (core == layer % 2))
            def _():
                cross_copy(layer, cross_turn.at[layer], s + 1 - 2 * core).wait_send()

    class Cascade:
        def __init__(self, blocks, send_sem, turn_sem, recv_sem):
            self.blocks, self.send_sem, self.turn_sem, self.recv_sem = blocks, send_sem, turn_sem, recv_sem

        def copy(self, src, layer, sem, to):
            return down(src, self.blocks.at[layer], sem, self.recv_sem.at[layer], to)

        def outgoing(self, src, act):
            for to in range(sections // 2 - 2, -1, -1):
                @pl.when(to < level)
                def _():
                    act(self.copy(src, s, self.send_sem.at[to], 2 * to + core))

            @pl.when(core == 1)
            def _():
                act(self.copy(src, s, self.send_sem.at[RING - 1], s - 1))

        def send(self, src):
            self.outgoing(src, lambda copy: copy.start())

        def relay(self):
            for layer in range(sections - 1, 1, -1):
                @pl.when((layer // 2 > level) & (core == layer % 2))
                def _():
                    block = self.blocks.at[layer]
                    self.copy(block, layer, self.turn_sem.at[layer], s + 1 - 2 * core).wait_recv()
                    self.copy(block, layer, self.turn_sem.at[layer], s + 1 - 2 * core).start()

        def rest(self):
            for layer in range(sections - 1, 0, -1):
                @pl.when((layer > s) & ((layer // 2 == level) | (core != layer % 2)))
                def _():
                    block = self.blocks.at[layer]
                    self.copy(block, layer, self.turn_sem.at[layer], s + 1 - 2 * core).wait_recv()

        def finish(self, src):
            self.outgoing(src, lambda copy: copy.wait_send())
            for layer in range(sections - 1, 1, -1):
                @pl.when((layer // 2 > level) & (core == layer % 2))
                def _():
                    self.copy(self.blocks.at[layer], layer, self.turn_sem.at[layer], s + 1 - 2 * core).wait_send()

    row_cascade = Cascade(rows_a, row_send, row_turn, row_recv)
    u_cascade = Cascade(u_all, u_send, u_turn_sem, u_recv)

    def near(src, dst, group, k):
        to = plane.slot(0, k, 0)
        return pltpu.make_async_remote_copy(
            src_ref=src, dst_ref=dst, send_sem=near_sem.at[group, 0], recv_sem=near_sem.at[group, k],
            device_id={"dp": to}, device_id_type=MESH,
        )

    def across(src, dst, group, k):
        to = wrap(level + k) * 2 + core
        return pltpu.make_async_remote_copy(
            src_ref=src, dst_ref=dst, send_sem=near_sem.at[group, 0], recv_sem=near_sem.at[group, k],
            device_id={"section": to}, device_id_type=MESH,
        )

    def twin(src, dst, group, k):
        return pltpu.make_async_remote_copy(
            src_ref=src, dst_ref=dst, send_sem=near_sem.at[group, 0], recv_sem=near_sem.at[group, k],
            device_id={"section": s + 1 - 2 * core}, device_id_type=MESH,
        )

    HOPS = (1, 3, 2)

    def top_copy(k):
        cols = pl.ds(
            pl.multiple_of((level * RING + wrap(x + k)) * width + core * (width // 2), width // 2), width // 2
        )
        return near(top_hbm.at[:, cols], merged.at[x, :, half_cols], 0, k)

    ring_gather.gather_send(1)
    for k in HOPS:
        top_copy(k).start()
    gather_a.round0()
    row_cascade.send(all_a.at[me])

    entries = list_ref.shape[1]
    chosen = [list_ref[0, i] for i in range(entries)]
    owners = [owner_ref[0, i] for i in range(entries)]
    keys = []
    for i in range(entries):
        place = jnp.int32(0)
        for j in range(i):
            place += (owners[j] == owners[i]).astype(jnp.int32)
        keys.append(owners[i] * CAP + place)
    lane = lax.broadcasted_iota(jnp.int32, ids_ref.shape[1:], 1)

    def fill_slot(owner, carry):
        row = jnp.full(ids_ref.shape[1:], -1, jnp.int32)
        for place in range(CAP):
            index = jnp.int32(-1)
            for i in range(entries):
                index = jnp.where(keys[i] == owner * CAP + place, chosen[i], index)
            slot_ref[owner * CAP + place] = index
            row = jnp.where(lane == place, jnp.where(index >= 0, me * tiles.shape[0] + index, -1), row)
        ids_ref[owner] = row
        return carry

    lax.fori_loop(0, GROUP, fill_slot, 0)
    swap_ids.start(lambda q: ids_ref.at[q], lambda k: ids_in.at[me])
    ids_in[me] = ids_ref[me]
    for layer in range(sections):
        @pl.when(layer <= s)
        def _():
            rows_a[layer] = jnp.zeros(rows_a.shape[1:], BF16)
    own_bt = own_b.T.astype(BF16)

    ring_gather.gather_wait(1)
    ring_gather.gather_send(2)
    gather_a.round1()

    def passed_on(k):
        spot = merged.at[wrap(x - k), :, half_cols]
        return twin(spot, spot, 1, k)

    for k in HOPS:
        spot = merged.at[wrap(x - k), :, half_cols]
        near(spot, spot, 0, k).wait_recv()
        passed_on(k).start()
    ring_gather.gather_wait(2)
    for k in HOPS:
        across(ring_b.at[wrap(level + k)], slice_b.at[level], 2, k).start()
    slice_b[level] = ring_b[level]

    row_cascade.relay()
    row_cascade.rest()
    for layer in range(sections):
        cross_part[layer * rank:(layer + 1) * rank] = jnp.dot(
            own_bt, rows_a[layer], preferred_element_type=F32
        ).astype(BF16)

    def piece(ref, q):
        return ref.at[pl.ds(pl.multiple_of(q * chunk, chunk), chunk)]

    swap_cross.start(lambda q: piece(cross_part, q), lambda k: cross_land.at[k - 1])
    gather_a.round2()

    loads[4].wait()
    other_cols = pl.ds(pl.multiple_of((1 - core) * (width // 2), width // 2), width // 2)
    for k in HOPS:
        spot = merged.at[wrap(x - k), :, other_cols]
        twin(spot, spot, 1, k).wait_recv()

    def direct(layer_level, dst):
        for spot in range(RING):
            dst[spot] = jnp.dot(merged[spot], slice_b[layer_level], preferred_element_type=F32).astype(BF16)

    for n, k in enumerate(HOPS):
        across(slice_b.at[wrap(level - k)], slice_b.at[wrap(level - k)], 2, k).wait_recv()
        direct(wrap(level - k), u_part.at[n])
        across(u_part.at[n], u_land.at[n], 3, RING - k).start()
    direct(level, u_part.at[RING - 1])
    gather_a.round3()

    swap_cross.wait_recv(cross_land)
    own_rows = pl.ds(pl.multiple_of(me * chunk, chunk), chunk)
    cross_sum = cross_part[own_rows].astype(F32)
    for k in range(GROUP - 1):
        cross_sum = cross_sum + cross_land[k].astype(F32)
    cross_all[s, own_rows] = (cross_sum * (scale_a * scale_b)).astype(BF16)
    spread_cross.start(lambda q: cross_all.at[s, own_rows], lambda k: cross_all.at[s, own_rows])

    gather_a.round4()
    loads[1].wait()

    def forward(left, blocks, q):
        cols = pl.ds(pl.multiple_of(q * width, width), width)
        return jnp.dot(left[:, cols], blocks[q], preferred_element_type=F32)

    acc[...] = jnp.zeros_like(acc)

    def forward_a(q, carry):
        acc[...] += forward(h_v, all_a, q)
        return carry

    lax.fori_loop(0, GROUP // 2, forward_a, 0)

    spread_cross.wait_recv(cross_all.at[s, pl.ds(0, (GROUP - 1) * chunk)])
    cross_outgoing(lambda copy: copy.start())

    for n, k in enumerate(HOPS):
        across(u_part.at[n], u_land.at[n], 3, RING - k).wait_recv()

    def turn(spot):
        summed = u_part[RING - 1, spot].astype(F32)
        for n in range(RING - 1):
            summed = summed + u_land[n, spot].astype(F32)
        return summed

    def u_copy(k):
        return near(u_turn.at[k - 1], u_near.at[k - 1], 4, k)

    for k in HOPS:
        u_turn[k - 1] = turn(wrap(x + k)).astype(BF16)
        u_copy(k).start()
    lax.fori_loop(GROUP // 2, GROUP, forward_a, 0)
    adapter_out = acc[...] * scale_a
    out_n[...] = adapter_out.astype(BF16)
    outs[level, x] = adapter_out.T.astype(BF16)
    for k in HOPS:
        near(outs.at[level, x], outs.at[level, x], 5, k).start()


    def backward(left, right, part, q):
        cols = pl.ds(pl.multiple_of(q * width, width), width)
        part[q] = jnp.dot(left, right[:, cols], preferred_element_type=F32).astype(BF16)

    order = [(2, 2)] + [(2, k) for k in (0, 1, 3)] + [(k, 2) for k in (0, 1, 3)]
    order += [(1, 1), (1, 3), (3, 1), (3, 3), (1, 0), (3, 0), (0, 1), (0, 3), (0, 0)]
    own_direct = turn(x)
    for k in HOPS:
        u_copy(k).wait_recv()
        own_direct = own_direct + u_near[k - 1].astype(F32)

    u_all[s] = (own_direct * scale_b).T.astype(BF16)
    u_cascade.send(u_all.at[s])
    for k in HOPS:
        spot = outs.at[level, wrap(x - k)]
        near(spot, spot, 5, k).wait_recv()
    for k in HOPS:
        across(outs.at[level], outs.at[level], 6, k).start()
    cross_relay()
    cross_rest()
    u_cascade.relay()
    u_cascade.rest()
    for layer in range(sections):
        @pl.when(layer >= s)
        def _():
            u_acc[layer] = u_all[layer].astype(F32)
    for layer in range(sections - 1, -1, -1):
        @pl.when(layer >= s)
        def _():
            delta = u_acc[layer].astype(BF16)
            deltas[layer] = delta
            for lower in range(layer):
                @pl.when(lower >= s)
                def _():
                    u_acc[lower] += jnp.dot(
                        cross_all[lower, layer * rank:(layer + 1) * rank], delta, preferred_element_type=F32
                    )

    for layer in range(sections):
        @pl.when(layer > s)
        def _():
            mixed_part[layer * rank:(layer + 1) * rank] = jnp.dot(
                deltas[layer], out_n[...], preferred_element_type=F32
            ).astype(BF16)

        @pl.when(layer <= s)
        def _():
            mixed_part[layer * rank:(layer + 1) * rank] = jnp.zeros((rank, rank), BF16)
    owns_rows = me * chunk // rank > s
    for k in range(1, GROUP):
        to = lax.rem(me + k, GROUP)

        @pl.when(to * chunk // rank > s)
        def _():
            swap_mixed.copy(piece(mixed_part, to), mixed_land.at[k - 1], to).start()

    for layer in range(sections):
        @pl.when(layer <= s)
        def _():
            mixed[layer * rank:(layer + 1) * rank] = jnp.zeros((rank, rank), BF16)

    def mixed_waits(wait):
        for layer in range(sections - 1):
            filled = (sections - 1 - layer) * rank

            @pl.when((s == layer) & owns_rows)
            def _():
                wait(mixed.at[pl.ds(0, filled - chunk)])

            @pl.when((s == layer) & jnp.logical_not(owns_rows))
            def _():
                wait(mixed.at[pl.ds(0, filled)])


    for dz, dx in order[:7]:
        backward(deltas[s], h_v, part_a, plane.away(dz, dx))
        scatter_a.send_chunk(dz, dx)

    def top_grad_of(layer_level):
        summed = jnp.dot(outs[layer_level, 0], merged[0], preferred_element_type=F32)
        for spot in range(1, RING):
            summed = summed + jnp.dot(outs[layer_level, spot], merged[spot], preferred_element_type=F32)
        return summed.astype(BF16)

    for n, k in enumerate(HOPS):
        spot = outs.at[wrap(level - k)]
        across(spot, spot, 6, k).wait_recv()
        grad_out[n] = top_grad_of(wrap(level - k))
        across(grad_out.at[n], part_b.at[level], 7, RING - k).start()
    part_b[level] = top_grad_of(level)
    for dz, dx in order[7:]:
        backward(deltas[s], h_v, part_a, plane.away(dz, dx))
        scatter_a.send_chunk(dz, dx)

    @pl.when(owns_rows)
    def _():
        swap_mixed.wait_recv(mixed_land)
        mixed_sum = mixed_part[own_rows].astype(F32)
        for k in range(GROUP - 1):
            mixed_sum = mixed_sum + mixed_land[k].astype(F32)
        mixed[own_rows] = mixed_sum.astype(BF16)
        spread_mixed.start(lambda q: mixed.at[own_rows], lambda k: mixed.at[own_rows])

    for a in (2, 1, 3, 0):
        scatter_a.pass_on(a)
    for k in HOPS:
        spot = part_b.at[wrap(level - k)]
        across(spot, spot, 7, k).wait_recv()
    ring_sum.sum_send()
    for a in (2, 1, 3, 0):
        scatter_a.settle(a)
    ring_sum.sum_pass()
    scatter_a.pass_last()
    mixed_waits(spread_mixed.wait_recv)
    loads[2].wait()
    loads[3].wait()

    def adam(which, gradient_of):
        for block in range(width // BS):
            rows = pl.ds(2 * BS * block + which, BS, stride=2)
            gradient = gradient_of(pl.ds(block * BS, BS))
            new_first = beta_one * m_v[rows, :] + (1.0 - beta_one) * gradient
            new_second = beta_two * v_v[rows, :] + (1.0 - beta_two) * gradient * gradient
            master = wide[rows, :]
            update = new_first / correct_one / (jnp.sqrt(new_second / correct_two) + adam_eps)
            fresh = master - learn_rate * (update + decay_rate * master)
            m_v[rows, :] = new_first
            v_v[rows, :] = new_second
            wide[rows, :] = fresh
            tiles[2 * block + which] = fresh.astype(BF16)

    relayed[...] = jnp.dot(rows_a[0], mixed[0:rank], preferred_element_type=F32)
    for layer in range(1, sections):
        relayed[...] += jnp.dot(
            rows_a[layer], mixed[layer * rank:(layer + 1) * rank], preferred_element_type=F32
        )
    ring_sum.sum_result(total)
    adam(1, lambda rows: (total[:, rows].T + relayed[rows] * scale_a) * scale_b)

    scatter_a.result(total)
    adam(0, lambda rows: total[:, rows].T * scale_a)

    for k in range(1, GROUP + 1):
        owner = lax.rem(me + k, GROUP)
        for place in range(CAP):
            index = slot_ref[owner * CAP + place]
            tile = tiles[jnp.maximum(index, 0)]
            outbox[owner, place] = jnp.where(index >= 0, tile, jnp.zeros_like(tile))
        if k < GROUP:
            swap_tiles.copy(outbox.at[owner], blocks_out.at[me], owner).start()
    kept = pltpu.make_async_copy(outbox.at[me], blocks_out.at[me], local_sem.at[5])
    kept.start()
    w_new[...] = wide[...].astype(BF16)
    stores = [
        pltpu.make_async_copy(src, dst, local_sem.at[k])
        for k, (src, dst) in enumerate(((w_new, w_out), (m_v, m_out), (v_v, v_out)))
    ]
    for store in stores:
        store.start()
    swap_ids.wait_recv(ids_in.at[pl.ds(0, GROUP - 1)])
    stores.append(pltpu.make_async_copy(ids_in, ids_out, local_sem.at[3]))
    stores[-1].start()

    gather_a.finish()
    ring_gather.finish()
    scatter_a.finish()
    ring_sum.finish()
    for group, whole in (
        (0, merged.at[pl.ds(0, RING - 1), :, half_cols]), (1, merged.at[pl.ds(0, RING - 1), :, half_cols]),
        (2, slice_b.at[pl.ds(0, RING - 1)]), (3, u_land), (4, u_near),
        (5, outs.at[0, pl.ds(0, RING - 1)]), (6, outs.at[pl.ds(0, RING - 1)]), (7, grad_out),
    ):
        near(whole, whole, group, 1).wait_send()
    row_cascade.finish(all_a.at[me])
    cross_finish()
    u_cascade.finish(u_all.at[s])
    swap_ids.wait_send(ids_ref.at[pl.ds(0, GROUP - 1)])
    swap_cross.wait_send(cross_land)
    mixed_waits(swap_mixed.wait_send)
    spread_cross.wait_send(mixed.at[pl.ds(0, (GROUP - 1) * chunk)])

    @pl.when(owns_rows)
    def _():
        spread_mixed.wait_send(mixed.at[pl.ds(0, (GROUP - 1) * chunk)])

    swap_tiles.wait_send(outbox.at[pl.ds(0, GROUP - 1)])
    swap_tiles.wait_recv(blocks_out.at[pl.ds(0, GROUP - 1)])
    kept.wait()
    for store in stores:
        store.wait()


def hand_over(
    w_in, m_in, v_in, blocks_in, ids_in, w_out, m_out, v_out, blocks_out, ids_out, w_v, m_v, v_v, blocks_v, in_sem, out_sem
):
    arrays = ((m_in, m_v, m_out), (v_in, v_v, v_out), (blocks_in, blocks_v, blocks_out), (w_in, w_v, w_out))
    fetches, stores = [], []
    for array, (src, stage, dst) in enumerate(arrays):
        half = src.shape[0] // 2
        for k in range(2):
            part = pl.ds(k * half, half)
            fetches.append(pltpu.make_async_copy(src.at[part], stage.at[part], in_sem.at[2 * array + k]))
            stores.append(pltpu.make_async_copy(stage.at[part], dst.at[part], out_sem.at[2 * array + k]))
    for fetch in fetches:
        fetch.start()
    ids_out[...] = ids_in[:, 0, :].T[:CAP, :]
    for fetch, store in zip(fetches, stores):
        fetch.wait()
        store.start()
    for store in stores:
        store.wait()


def shards(section_inputs, top_grad, weights, first_moment, second_moment, block_list, block_owner):
    sections = lax.axis_size("section")
    model_width = section_inputs.shape[3]
    rank = weights.shape[3]
    width = weights.shape[1]
    tokens = section_inputs.shape[1] * section_inputs.shape[2]
    chunk = sections * rank // GROUP
    entries = block_list.shape[2]
    scale_a = model_width ** (-0.5)
    scale_b = rank ** (-0.5)

    any_spec = pl.BlockSpec(memory_space=pl.ANY)
    vmem = pl.BlockSpec(memory_space=pltpu.VMEM)
    dma = pltpu.SemaphoreType.DMA
    new_weights, new_first, new_second, blocks, got_ids = pl.pallas_call(
        functools.partial(whole_kernel, sections, scale_a, scale_b),
        out_shape=(
            jax.ShapeDtypeStruct((2 * width, rank), BF16),
            jax.ShapeDtypeStruct((2 * width, rank), F32),
            jax.ShapeDtypeStruct((2 * width, rank), F32),
            jax.ShapeDtypeStruct((GROUP, CAP, BS, BS), BF16),
            jax.ShapeDtypeStruct((GROUP, 8, 128), jnp.int32),
        ),
        in_specs=[any_spec] * 5 + [pl.BlockSpec(memory_space=pltpu.SMEM)] * 2,
        out_specs=(any_spec,) * 5,
        scratch_shapes=[
            pltpu.VMEM((tokens, model_width), BF16),
            pltpu.VMEM((2 * width, rank), BF16),
            pltpu.VMEM((2 * width, rank), F32),
            pltpu.VMEM((2 * width, rank), F32),
            pltpu.VMEM((2 * width, rank), F32),
            pltpu.VMEM((GROUP, width, rank), BF16),
            pltpu.VMEM((GROUP, rank, width), BF16),
            pltpu.VMEM((60, rank // 4, width), BF16),
            pltpu.VMEM((RING, width, rank), BF16),
            pltpu.VMEM((RING, width, rank), BF16),
            pltpu.VMEM((RING, tokens, width), BF16),
            pltpu.VMEM((RING, RING, tokens, rank), BF16),
            pltpu.VMEM((RING - 1, RING, tokens, rank), BF16),
            pltpu.VMEM((RING - 1, tokens, rank), BF16),
            pltpu.VMEM((RING - 1, tokens, rank), BF16),
            pltpu.VMEM((RING, RING, rank, tokens), BF16),
            pltpu.VMEM((RING - 1, rank, width), BF16),
            pltpu.VMEM((RING, rank, width), BF16),
            pltpu.VMEM((6, rank // 2, width), BF16),
            pltpu.VMEM((sections, width, rank), BF16),
            pltpu.VMEM((sections, sections * rank, rank), BF16),
            pltpu.VMEM((sections * rank, rank), BF16),
            pltpu.VMEM((GROUP - 1, chunk, rank), BF16),
            pltpu.VMEM((sections * rank, rank), BF16),
            pltpu.VMEM((GROUP - 1, chunk, rank), BF16),
            pltpu.VMEM((sections * rank, rank), BF16),
            pltpu.VMEM((tokens, rank), F32),
            pltpu.VMEM((tokens, rank), BF16),
            pltpu.VMEM((sections, rank, tokens), BF16),
            pltpu.VMEM((sections, rank, tokens), F32),
            pltpu.VMEM((sections, rank, tokens), BF16),
            pltpu.VMEM((rank, width), F32),
            pltpu.VMEM((width, rank), F32),
            pltpu.VMEM((2 * width // BS, BS, BS), BF16),
            pltpu.VMEM((GROUP, CAP, BS, BS), BF16),
            pltpu.VMEM((2 * width, rank), BF16),
            pltpu.VMEM((GROUP, 8, 128), jnp.int32),
            pltpu.VMEM((GROUP, 8, 128), jnp.int32),
            pltpu.SMEM((GROUP * CAP,), jnp.int32),
            dma((6,)),
            dma((1,)), dma((40,)), dma((1,)), dma((4,)),
            dma((1,)), dma((60,)), dma((1,)), dma((6,)),
            dma((RING,)), dma((sections,)), dma((sections,)),
            dma((RING,)), dma((sections,)), dma((sections,)),
            dma((RING,)), dma((sections,)), dma((sections,)),
            dma((6, 2)), dma((8, RING)),
        ],
        compiler_params=pltpu.CompilerParams(
            collective_id=0, has_side_effects=True, vmem_limit_bytes=62 * 1024 * 1024
        ),
        cost_estimate=pl.CostEstimate(
            flops=8 * tokens * model_width * rank, bytes_accessed=4 * tokens * model_width, transcendentals=0
        ),
    )(
        section_inputs.reshape(tokens, model_width),
        top_grad.reshape(tokens, model_width),
        weights.reshape(2 * width, rank),
        first_moment.reshape(2 * width, rank),
        second_moment.reshape(2 * width, rank),
        block_list.reshape(1, entries),
        block_owner.reshape(1, entries),
    )
    results = (new_weights, new_first, new_second, blocks)
    *results, got_ids = pl.pallas_call(
        hand_over,
        out_shape=(
            *(jax.ShapeDtypeStruct(array.shape, array.dtype) for array in results),
            jax.ShapeDtypeStruct((CAP, GROUP), jnp.int32),
        ),
        in_specs=[any_spec] * 4 + [vmem],
        out_specs=(any_spec,) * 4 + (vmem,),
        scratch_shapes=[pltpu.VMEM(array.shape, array.dtype) for array in results] + [dma((8,)), dma((8,))],
    )(*results, got_ids)
    new_weights, new_first, new_second, blocks = results
    return (
        new_weights.reshape(weights.shape),
        new_first.reshape(weights.shape),
        new_second.reshape(weights.shape),
        blocks[None, None],
        got_ids.T[None, None],
    )


def solution(mesh):
    placed = (
        P("section", None, "dp", None),
        P(None, "dp", None),
        P("section", "dp", None, None),
        P("section", "dp", None, None),
        P("section", "dp", None, None),
        P("section", "dp", None),
        P("section", "dp", None, None),
    )
    return jax.shard_map(
        shards,
        mesh=mesh,
        in_specs=placed,
        out_specs=(
            P("section", "dp", None, None),
            P("section", "dp", None, None),
            P("section", "dp", None, None),
            P("section", "dp", None, None, None, None),
            P("section", "dp", None, None),
        ),
        check_vma=False,
    )
```
